512 devices in a mesh: slab: 64 (over z, x_hi, core), col: 8 (over x_lo, y).
Axes of the slice: x: 4 (x_hi: 2, x_lo: 2; x = x_hi * 2 + x_lo), y: 4, z: 16, core: 2. Of those that a mesh axis runs over, the one named last changes fastest.
Arguments:
- positions: float32 [3, 4194304], P(None, ('slab', 'col')), may hold values from -3 to 3
- mass: float32 [4194304], P(('slab', 'col')), may hold values from 0.5 to 2
- smooth: float32 [4194304], P(('slab', 'col')), may hold values from 0.6 to 1.6
- cell_y: int32 [4194304], P(('slab', 'col')), may hold values from 0 to 127
- cell_z: int32 [4194304], P(('slab', 'col')), may hold values from 0 to 1023
- cic_frac: float32 [3, 4194304], P(None, ('slab', 'col')), may hold values from 0 to 1
- pair_blocks: int32 [32768, 9], P(('slab', 'col')), may hold values from 0 to 127, as said below
- pair_count: int32 [32768], P(('slab', 'col')), may hold values from 3 to 9, as said below
Outputs:
- density: float32 [4194304], P(('slab', 'col'))
- acceleration: float32 [3, 4194304], P(None, ('slab', 'col'))
- mesh_mass: float32 [128, 1024, 1024], P('slab', 'col')
The draws below stay inside these ranges and needn't reach their ends.
Inputs may be any that keep to these rules, and one draw needn't show every extreme that they name: `pair_blocks`: slot 0 of block b names b itself (index 32 + b mod 64), slot 1 the block 32 before it and slot 2 the block 32 after it; every entry lies within 32 blocks of the block itself, live entries of a row are distinct, dead slots repeat slot 0. `pair_count`: the first block of every device has all 9 slots live.
All inputs are finite; a program needn't handle non-finite values.
Results may differ from the reference program's by a relative error of at most 0.0037.
Values sent between devices are 32-bit elements; how exact they have to be, the bound alone decides.
No kernel may reach another device: no remote copies, remote signals or barrier semaphores. Data moves between devices by JAX's collectives and lax.ppermute only.
A program may use at most 64 MiB of HBM per device.

```python
import math
import jax
import jax.numpy as jnp
from jax import lax

BLK = 128
CB = 64
NP = 9
XP = 2
MYD = 128
MZ = 1024
HB = 32
PARTICLES = 4194304
BLOCKS = 32768
MX = 128
MY = 1024
N_SLAB = 64
N_COL = 8


def partner_table(key):
    span = 2 * HB - 2
    offsets = jnp.concatenate([jnp.arange(-HB + 1, 0), jnp.arange(1, HB)]).astype(jnp.int32)
    scores = jax.random.randint(key, (BLOCKS, span), 0, 1 << 20) * span + jnp.arange(span)[None, :]
    order = jnp.argsort(scores, axis=1)
    picked = offsets[order[:, :NP - 3]]
    local = (jnp.arange(BLOCKS) % CB).astype(jnp.int32)
    centre = (HB + local)[:, None]
    table = jnp.concatenate([centre, centre - HB, centre + HB, centre + picked], axis=1)
    count = jax.random.randint(jax.random.fold_in(key, 5), (BLOCKS,), 3, NP + 1)
    count = jnp.where(local == 0, NP, count)
    table = jnp.where(jnp.arange(NP)[None, :] < count[:, None], table, centre)
    return (table.astype(jnp.int32), count.astype(jnp.int32))


def draw_pair_blocks(key, part):
    return partner_table(key)[0]


def draw_pair_count(key, part):
    return partner_table(key)[1]


def with_ends(array, own_key, low, top_value):
    spot = [jax.random.randint(jax.random.fold_in(own_key, axis), (), 0, length) for axis, length in enumerate(array.shape)]
    widest = array.shape.index(max(array.shape))
    next_to = spot[:widest] + [(spot[widest] + 1) % array.shape[widest]] + spot[widest + 1:]
    return array.at[tuple(spot)].set(low).at[tuple(next_to)].set(top_value)


def level_of(stream_key, shape, pieces, low, largest):
    loudness = 1.0
    for axis_at, parts in pieces:
        heights = jax.random.uniform(jax.random.fold_in(jax.random.fold_in(stream_key, 6), axis_at), (parts,), jnp.float32, low / len(pieces), largest / len(pieces))
        loudness = loudness * jnp.repeat(jnp.exp(heights), shape[axis_at] // parts).reshape((-1,) + (1,) * (len(shape) - 1 - axis_at))
    return loudness


def centred(own_key, extent, scale, limit, split=(), held_as=jnp.bfloat16):
    values = jax.random.normal(own_key, extent, jnp.float32) * scale
    if len(split) > 0:
        values = level_of(own_key, extent, split, -0.22, 0.18) * values
    return jnp.clip(values, min=-limit, max=limit).astype(held_as)


def setup_inputs(seed: int = 0) -> dict:
    key_of = jax.random.split(jax.random.key(seed), 9)
    return {
        "positions": centred(key_of[0], (3, PARTICLES), 0.5, 3.0, ((1, 512),), jnp.float32),
        "mass": jnp.clip(jnp.exp(math.log(2.0) - 1.3862944 * jax.random.uniform(key_of[1], (PARTICLES,), jnp.float32) ** level_of(key_of[1], (PARTICLES,), ((0, 512),), -0.2, 0.2)), 0.5, 2.0),
        "smooth": jnp.clip(jnp.exp(math.log(1.6) - 0.98082923 * jax.random.uniform(key_of[2], (PARTICLES,), jnp.float32) ** level_of(key_of[2], (PARTICLES,), ((0, 512),), -0.2, 0.2)), 0.6, 1.6),
        "cell_y": with_ends(jax.random.randint(key_of[3], (PARTICLES,), 0, MYD), jax.random.fold_in(key_of[3], 1), 0, MYD - 1).astype(jnp.int32),
        "cell_z": with_ends(jax.random.randint(key_of[4], (PARTICLES,), 0, MZ), jax.random.fold_in(key_of[4], 1), 0, MZ - 1).astype(jnp.int32),
        "cic_frac": jnp.clip(1.0 * jax.random.uniform(key_of[5], (3, PARTICLES), jnp.float32) ** level_of(key_of[5], (3, PARTICLES), ((1, 512),), -0.2, 0.2), 0.0, 1.0),
        "pair_blocks": draw_pair_blocks(jax.random.fold_in(key_of[8], 71), 0),
        "pair_count": draw_pair_count(jax.random.fold_in(key_of[8], 71), 0),
    }


def block_density(own_rows, partner_rows, slot_keep):
    distance_sq = sum((own_rows[component][:, :, None, None] - partner_rows[component][:, None, :, :]) ** 2 for component in range(3))
    kernel = jnp.exp(-distance_sq / (own_rows[4] ** 2)[:, :, None, None])
    weights = partner_rows[3] * slot_keep[:, :, None]
    return jnp.sum(kernel * weights[:, None, :, :], axis=(2, 3)) * (1.0 / (NP * BLK))


def block_force(own_rows, partner_rows, slot_keep, own_term, partner_term):
    separations = [own_rows[component][:, :, None, None] - partner_rows[component][:, None, :, :] for component in range(3)]
    distance_sq = separations[0] ** 2 + separations[1] ** 2 + separations[2] ** 2
    spread = 0.5 * ((own_rows[4] ** 2)[:, :, None, None] + (partner_rows[4] ** 2)[:, None, :, :])
    weights = partner_rows[3] * slot_keep[:, :, None]
    factor = jnp.exp(-distance_sq / spread) / spread * (own_term[:, :, None, None] + partner_term[:, None, :, :]) * weights[:, None, :, :] * (2.0 / (NP * BLK))
    return jnp.stack([jnp.sum(factor * separation, axis=(2, 3)) for separation in separations])


def reference(positions, mass, smooth, cell_y, cell_z, cic_frac, pair_blocks, pair_count):
    devices = N_SLAB * N_COL
    state = jnp.concatenate([positions, mass[None], smooth[None]], axis=0).reshape(5, devices, CB, BLK)
    device_ids = jnp.arange(devices)
    lower = ((device_ids // N_COL - 1) % N_SLAB) * N_COL + device_ids % N_COL
    upper = ((device_ids // N_COL + 1) % N_SLAB) * N_COL + device_ids % N_COL
    tables = pair_blocks.reshape(devices, CB, NP)
    counts = pair_count.reshape(devices, CB)

    def extend(blocks, device):
        return jnp.concatenate([blocks[:, lower[device], CB - HB:], blocks[:, device], blocks[:, upper[device], :HB]], axis=1)

    def slot_mask(device):
        return (jnp.arange(NP)[None, :] < counts[device][:, None]).astype(jnp.float32)

    def density_of(device):
        extended = extend(state, device)
        return block_density(state[:, device], extended[:, tables[device]], slot_mask(device))

    density = lax.map(density_of, device_ids)
    term = density ** (-1.0 / 3.0)

    def force_of(device):
        extended = extend(state, device)
        term_ext = extend(term[None], device)[0]
        return block_force(state[:, device], extended[:, tables[device]], slot_mask(device), term[device], term_ext[tables[device]])

    acceleration = lax.map(force_of, device_ids)
    acceleration = jnp.moveaxis(acceleration, 1, 0).reshape(3, PARTICLES)

    particle_ids = jnp.arange(PARTICLES)
    owner = particle_ids // (CB * BLK)
    block_local = (particle_ids % (CB * BLK)) // BLK
    plane = (owner // N_COL) * XP + block_local // (CB // XP)
    column = (owner % N_COL) * MYD + cell_y
    grid = jnp.zeros((MX, MY, MZ), jnp.float32)
    for shift_x in (0, 1):
        weight_x = cic_frac[0] if shift_x else 1.0 - cic_frac[0]
        for shift_y in (0, 1):
            weight_y = cic_frac[1] if shift_y else 1.0 - cic_frac[1]
            loads = lax.optimization_barrier(((mass * weight_x) * weight_y).astype(jnp.bfloat16)).astype(jnp.float32)
            for shift_z in (0, 1):
                weight_z = cic_frac[2] if shift_z else 1.0 - cic_frac[2]
                depth = lax.optimization_barrier(weight_z.astype(jnp.bfloat16)).astype(jnp.float32)
                grid = grid.at[(plane + shift_x) % MX, (column + shift_y) % MY, (cell_z + shift_z) % MZ].add(loads * depth)
    return density.reshape(PARTICLES), acceleration, grid
```

```python
import functools
import jax
import jax.numpy as jnp
from jax import lax
from jax.sharding import PartitionSpec as P
from jax.experimental import pallas as pl
from jax.experimental.pallas import tpu as pltpu

BLK=128; NP=9; XP=2; MYD=128; MZ=1024
LOG2E=1.4426950408889634
f32=jnp.float32; bf16=jnp.bfloat16

def split3(x):
    h=x.astype(bf16).astype(f32)
    r=x-h
    m=r.astype(bf16).astype(f32)
    l=(r-m)
    return h,m,l

def feats(st):
    x=st[0:3]; m=st[3:4]; s=st[4:5]
    n=x[0:1]*x[0:1]+x[1:2]*x[1:2]+x[2:3]*x[2:3]
    one=jnp.ones_like(m)
    return x,n,m,s,one

def stack_a(h,m,l):
    z=jnp.zeros((80,h.shape[1]),f32)
    return jnp.concatenate([h,h,m,m,h,l,z],0)
def stack_b(h,m,l):
    z=jnp.zeros((80,h.shape[1]),f32)
    return jnp.concatenate([h,m,h,m,l,h,z],0)

def build_list(pb,pc,lst,G,count):
    def body(b,pos):
        for k in range(NP):
            lst[pos+k]=pb[b,k]+b*256
        return pos+pc[b]
    n=lax.fori_loop(0,count,body,jnp.int32(0))
    for k in range(G):
        lst[n+k]=jnp.int32(count*256)
    return (n+G-1)//G

def prep_a(src,a_ref,at,nb):
    def body(i,_):
        st=src[:,pl.ds(pl.multiple_of(i*128,128),128)]
        x,n,m,s,one=feats(st)
        s8=jnp.concatenate([x,n,jnp.log2(m),0.5*s*s,one,jnp.zeros_like(one)],0)
        a=stack_a(*split3(s8))
        a_ref[at+i]=a.T.astype(bf16)
        return 0
    lax.fori_loop(0,nb,body,0,unroll=4)

def density_kernel(G,own,lo,hi,pb,pc,den,term,a_ref,b_ref,acc,lst):
    nb=den.shape[0]; hb=nb//2
    nit=build_list(pb,pc,lst,G,nb)
    prep_a(lo,a_ref,0,hb); prep_a(own,a_ref,hb,nb); prep_a(hi,a_ref,hb+nb,hb)
    def bb(i,_):
        st=own[:,pl.ds(pl.multiple_of(i*128,128),128)]
        x,n,m,s,one=feats(st)
        c=LOG2E/(s*s)
        b8=jnp.concatenate([2*c*x,-c,one,jnp.zeros_like(one),-c*n,jnp.zeros_like(one)],0)
        b_ref[i]=stack_b(*split3(b8)).astype(bf16)
        return 0
    lax.fori_loop(0,nb,bb,0,unroll=4)
    b_ref[nb]=jnp.zeros((128,128),bf16)
    acc[...]=jnp.zeros_like(acc)
    def main(it,_):
        for g in range(G):
            code=lst[it*G+g]
            b=code>>8; p=code&255
            e=jnp.dot(a_ref[p],b_ref[b],preferred_element_type=f32)
            q=jnp.exp2(e)
            acc[b]+=q.reshape(16,8,128).sum(0)
        return 0
    lax.fori_loop(0,nit,main,0)
    d=acc[0:nb].sum(1)*(1.0/(NP*BLK))
    den[...]=d
    term[...]=jnp.exp2(jnp.log2(d)*(-1.0/3.0))

def density(own,lo,hi,pb,pc,G=8):
    nb=pb.shape[0]
    V=pl.BlockSpec(memory_space=pltpu.VMEM); S=pl.BlockSpec(memory_space=pltpu.SMEM)
    return pl.pallas_call(functools.partial(density_kernel,G),
        out_shape=[jax.ShapeDtypeStruct((nb,128),f32)]*2,
        in_specs=[V,V,V,S,S],out_specs=[V,V],
        scratch_shapes=[pltpu.VMEM((2*nb,128,128),bf16),pltpu.VMEM((nb+1,128,128),bf16),pltpu.VMEM((nb+1,8,128),f32),
                        pltpu.SMEM((nb*NP+NP+2*G,),jnp.int32)],
        compiler_params=pltpu.CompilerParams(vmem_limit_bytes=48<<20),
        name="density")(own,lo,hi,pb,pc)

def force_kernel(G,own,lo,hi,town,tlo,thi,pb,pc,out,a_ref,b_ref,v_ref,acc,lst):
    nb=town.shape[0]; hb=nb//2
    nit=build_list(pb,pc,lst,G,nb)
    prep_a(lo,a_ref,0,hb); prep_a(own,a_ref,hb,nb); prep_a(hi,a_ref,hb+nb,hb)
    def pv(src,t,at,n_):
        def body(i,_):
            st=src[:,pl.ds(pl.multiple_of(i*128,128),128)]
            x=st[0:3]; m=st[3:4]
            mt=m*t[pl.ds(i,1),:]
            v=jnp.concatenate([m,m*x,mt,mt*x],0)
            h=v.astype(bf16)
            l=(v-h.astype(f32)).astype(bf16)
            v_ref[at+i]=jnp.concatenate([h.astype(f32),l.astype(f32)],0).astype(bf16)
            return 0
        lax.fori_loop(0,n_,body,0,unroll=4)
    pv(lo,tlo,0,hb); pv(own,town,hb,nb); pv(hi,thi,hb+nb,hb)
    def bb(i,_):
        st=own[:,pl.ds(pl.multiple_of(i*128,128),128)]
        x,n,m,s,one=feats(st)
        z=jnp.zeros_like(one)
        b8=jnp.concatenate([(2*LOG2E)*x,-LOG2E*one,z,z,-LOG2E*n,z],0)
        c8=jnp.concatenate([z,z,z,z,z,one,0.5*s*s,z],0)
        b_ref[i,:,0:128]=stack_b(*split3(b8)).astype(bf16)
        b_ref[i,:,128:256]=stack_b(*split3(c8)).astype(bf16)
        return 0
    lax.fori_loop(0,nb,bb,0,unroll=4)
    b_ref[nb]=jnp.ones((128,256),bf16)
    acc[...]=jnp.zeros_like(acc)
    def main(it,_):
        L=4
        cs=[lst[it*G+g] for g in range(G)]
        qs={}; es={}
        def d1(g):
            es[g]=jnp.dot(a_ref[cs[g]&255],b_ref[cs[g]>>8],preferred_element_type=f32)
        def qq(g):
            e=es.pop(g)
            rs=pl.reciprocal(e[:,128:256],approx=True)
            qs[g]=(jnp.exp2(e[:,0:128]*rs)*rs).astype(bf16)
        def d2(g):
            acc[cs[g]>>8]+=jnp.dot(v_ref[cs[g]&255],qs.pop(g),preferred_element_type=f32)
        for s in range(G+2*L):
            if s<G: d1(s)
            if 0<=s-L<G: qq(s-L)
            if 0<=s-2*L<G: d2(s-2*L)
        return 0
    lax.fori_loop(0,nit,main,0)
    def fin(i,_):
        a=acc[i]
        s8=a[0:8]+a[8:16]
        x=own[0:3,pl.ds(pl.multiple_of(i*128,128),128)]
        t=town[pl.ds(i,1),:]
        f=t*(x*s8[0:1]-s8[1:4])+(x*s8[4:5]-s8[5:8])
        out[:,pl.ds(pl.multiple_of(i*128,128),128)]=f*(2.0/(NP*BLK))
        return 0
    lax.fori_loop(0,nb,fin,0,unroll=4)

def force(own,lo,hi,town,tlo,thi,pb,pc,G=8):
    nb=pb.shape[0]
    V=pl.BlockSpec(memory_space=pltpu.VMEM); S=pl.BlockSpec(memory_space=pltpu.SMEM)
    return pl.pallas_call(functools.partial(force_kernel,G),
        out_shape=jax.ShapeDtypeStruct((3,nb*128),f32),
        in_specs=[V]*6+[S,S],out_specs=V,
        scratch_shapes=[pltpu.VMEM((2*nb,128,128),bf16),pltpu.VMEM((nb+1,128,256),bf16),pltpu.VMEM((2*nb,16,128),bf16),
                        pltpu.VMEM((nb+1,16,128),f32),
                        pltpu.SMEM((nb*NP+NP+2*G,),jnp.int32)],
        compiler_params=pltpu.CompilerParams(vmem_limit_bytes=48<<20),
        name="force")(own,lo,hi,town,tlo,thi,pb,pc)
i16=jnp.int16

def depth_table(iz,cz,fz,kc):
    a=cz.astype(i16); b=((cz+1)&(MZ-1)).astype(i16)
    w0=(1.0-fz).astype(bf16); w1=fz.astype(bf16)
    return jnp.where(iz==a,w0,jnp.where(iz==b,w1,jnp.zeros_like(w1)))

def plane_rows(iy,cy,w_lo,w_hi):
    a=cy.astype(i16); b=(cy+1).astype(i16)
    z=jnp.zeros_like(w_lo)
    return jnp.where(iy==a,w_lo,jnp.where(iy==b,w_hi,z))

def deposit_own_kernel(kc,st,grid,rim):
    n=st.shape[1]; half=n//2
    iz=lax.broadcasted_iota(i16,(MZ,kc),0)
    iy=lax.broadcasted_iota(i16,(128,kc),0)
    def parts(at):
        s=st[:,pl.ds(at,kc)]
        m=s[3:4]; cy=s[5:6].astype(jnp.int32); cz=s[6:7].astype(jnp.int32)
        return m,cy,cz,s[7:8],s[8:9],s[9:10]
    def rowset(m,wx,cy,fy):
        mx=m*wx
        lo=(mx*(1.0-fy)).astype(bf16); hi=(mx*fy).astype(bf16)
        main=plane_rows(iy,cy,lo,hi)
        edge=jnp.where(cy.astype(i16)==127,hi,jnp.zeros_like(hi))
        return main,edge
    grid[...]=jnp.zeros_like(grid); rim[...]=jnp.zeros_like(rim)
    nt=(((1,),(1,)),((),()))
    it=lax.broadcasted_iota(i16,(16,kc),0)
    def first(i,_):
        m,cy,cz,fx,fy,fz=parts(pl.multiple_of(i*kc,128))
        d=depth_table(iz,cz,fz,kc)
        a0,e0=rowset(m,1.0-fx,cy,fy)
        a1,e1=rowset(m,fx,cy,fy)
        zz=jnp.zeros_like(it).astype(bf16)
        ed=jnp.where(it==0,e0,jnp.where(it==1,e1,zz))
        l=jnp.concatenate([a0,a1,ed],0)
        u=lax.dot_general(l,d,nt,preferred_element_type=f32)
        grid[0]+=u[0:128]; grid[1]+=u[128:256]; rim[...]+=u[256:264]
        return 0
    lax.fori_loop(0,half//kc,first,0)
    def second(i,_):
        m,cy,cz,fx,fy,fz=parts(pl.multiple_of(half+i*kc,128))
        d=depth_table(iz,cz,fz,kc)
        a1,e1=rowset(m,1.0-fx,cy,fy)
        zz=jnp.zeros_like(it).astype(bf16)
        l=jnp.concatenate([a1,jnp.where(it==1,e1,zz)],0)
        u=lax.dot_general(l,d,nt,preferred_element_type=f32)
        grid[1]+=u[0:128]; rim[...]+=u[128:136]
        return 0
    lax.fori_loop(0,half//kc,second,0)

def deposit_in_kernel(kc,st,g_in,r_in,grid,rim):
    n=st.shape[1]
    iz=lax.broadcasted_iota(i16,(MZ,kc),0)
    iy=lax.broadcasted_iota(i16,(128,kc),0)
    nt=(((1,),(1,)),((),()))
    it=lax.broadcasted_iota(i16,(16,kc),0)
    grid[...]=g_in[...]; rim[...]=r_in[...]
    def body(i,_):
        s=st[:,pl.ds(pl.multiple_of(i*kc,128),kc)]
        m=s[3:4]; cy=s[5:6].astype(jnp.int32); cz=s[6:7].astype(jnp.int32)
        mx=m*s[7:8]; fy=s[8:9]
        lo=(mx*(1.0-fy)).astype(bf16); hi=(mx*fy).astype(bf16)
        d=depth_table(iz,cz,s[9:10],kc)
        a=plane_rows(iy,cy,lo,hi)
        e=jnp.where(cy.astype(i16)==127,hi,jnp.zeros_like(hi))
        zz=jnp.zeros_like(it).astype(bf16)
        l=jnp.concatenate([a,jnp.where(it==0,e,zz)],0)
        u=lax.dot_general(l,d,nt,preferred_element_type=f32)
        grid[0]+=u[0:128]; rim[...]+=u[128:136]
        return 0
    lax.fori_loop(0,n//kc,body,0)

V=pl.BlockSpec(memory_space=pltpu.VMEM)
def deposit_own(st,kc=512,name="dep_own"):
    return pl.pallas_call(functools.partial(deposit_own_kernel,kc),
        out_shape=[jax.ShapeDtypeStruct((2,128,MZ),f32),jax.ShapeDtypeStruct((8,MZ),f32)],
        in_specs=[V],out_specs=[V,V],
        compiler_params=pltpu.CompilerParams(vmem_limit_bytes=48<<20),name=name)(st)
def deposit_in(st,g,r,kc=512,name="dep_in"):
    return pl.pallas_call(functools.partial(deposit_in_kernel,kc),
        out_shape=[jax.ShapeDtypeStruct((2,128,MZ),f32),jax.ShapeDtypeStruct((8,MZ),f32)],
        in_specs=[V,V,V],out_specs=[V,V],
        compiler_params=pltpu.CompilerParams(vmem_limit_bytes=48<<20),name=name)(st,g,r)


def on_device(positions, mass, smooth, cell_y, cell_z, cic_frac, pair_blocks, pair_count):
    half = mass.shape[0] // 2
    hb = pair_blocks.shape[0] // 2
    state = jnp.concatenate(
        [positions, mass[None], smooth[None], cell_y.astype(f32)[None], cell_z.astype(f32)[None], cic_frac], axis=0
    )
    slabs = lax.axis_size("slab")
    cols = lax.axis_size("col")
    up = [(i, (i + 1) % slabs) for i in range(slabs)]
    down = [((i + 1) % slabs, i) for i in range(slabs)]
    right = [(i, (i + 1) % cols) for i in range(cols)]
    lo = lax.ppermute(state[:, half:], "slab", up)
    hi = lax.ppermute(state[:5, :half], "slab", down)
    grid, rim = deposit_own(state, 1024)
    den, term = density(state, lo, hi, pair_blocks, pair_count, 32)
    tlo = lax.ppermute(term[hb:], "slab", up)
    thi = lax.ppermute(term[:hb], "slab", down)
    grid, rim = deposit_in(lo, grid, rim, 1024)
    rows = lax.ppermute(rim[:2], "col", right)
    acc = force(state, lo, hi, term, tlo, thi, pair_blocks, pair_count, 16)
    grid = grid.at[:, 0].add(rows)
    return den.reshape(-1), acc, grid


def solution(mesh):
    return jax.shard_map(
        on_device,
        mesh=mesh,
        in_specs=(
            P(None, ("slab", "col")),
            P(("slab", "col")),
            P(("slab", "col")),
            P(("slab", "col")),
            P(("slab", "col")),
            P(None, ("slab", "col")),
            P(("slab", "col"), None),
            P(("slab", "col")),
        ),
        out_specs=(P(("slab", "col")), P(None, ("slab", "col")), P("slab", "col", None)),
        check_vma=False,
    )
```

```python
import functools

import jax
import jax.numpy as jnp
from jax import lax
from jax.experimental import pallas as pl
from jax.experimental.pallas import tpu as pltpu
from jax.sharding import PartitionSpec as P

BLK = 128
NP = 9
XP = 2
MYD = 128
MZ = 1024
LOG2E = 1.4426950408889634
KF = 48
GROUP = 32
SPAN = 1024

f32 = jnp.float32
bf16 = jnp.bfloat16
i16 = jnp.int16
i32 = jnp.int32

VM = pl.BlockSpec(memory_space=pltpu.VMEM)
SM = pl.BlockSpec(memory_space=pltpu.SMEM)
AN = pl.BlockSpec(memory_space=pl.ANY)
HB = pl.BlockSpec(memory_space=pltpu.HBM)
NT = (((1,), (1,)), ((), ()))


def lanes(i, width=BLK):
    return pl.ds(pl.multiple_of(i * width, BLK), width)


def pack_kernel(pos, mass, smooth, cy, cz, frac, pairs, counts, own, tail, head, vpairs, vcounts, vpos, vmass, vsmooth, vcy, vcz, vfrac, sems):
    half = own.shape[1] // 2
    moves = (
        (pos, vpos),
        (mass, vmass),
        (smooth, vsmooth),
        (cy, vcy),
        (cz, vcz),
        (frac, vfrac),
        (pairs, vpairs),
        (counts, vcounts),
    )
    copies = [pltpu.make_async_copy(src, dst, sems.at[k]) for k, (src, dst) in enumerate(moves)]
    for copy in copies:
        copy.start()
    for copy in copies:
        copy.wait()
    own[0:3] = vpos[...]
    own[3:4] = vmass[...]
    own[4:5] = vsmooth[...]
    own[5:6] = vcy[...].astype(f32)
    own[6:7] = vcz[...].astype(f32)
    own[7:10] = vfrac[...]
    tail[...] = own[:, half:]
    head[...] = own[0:5, :half]


def pack(positions, mass, smooth, cell_y, cell_z, cic_frac, pairs, counts):
    n = mass.shape[0]
    nb = counts.shape[0]
    return pl.pallas_call(
        pack_kernel,
        out_shape=[
            jax.ShapeDtypeStruct((10, n), f32),
            jax.ShapeDtypeStruct((10, n // 2), f32),
            jax.ShapeDtypeStruct((5, n // 2), f32),
            jax.ShapeDtypeStruct((NP, nb), i32),
            jax.ShapeDtypeStruct((1, nb), i32),
        ],
        in_specs=[HB] * 8,
        out_specs=[VM] * 5,
        scratch_shapes=[
            pltpu.VMEM((3, n), f32),
            pltpu.VMEM((1, n), f32),
            pltpu.VMEM((1, n), f32),
            pltpu.VMEM((1, n), i32),
            pltpu.VMEM((1, n), i32),
            pltpu.VMEM((3, n), f32),
            pltpu.SemaphoreType.DMA((8,)),
        ],
        name="pack",
    )(positions, mass[None], smooth[None], cell_y[None], cell_z[None], cic_frac, pairs, counts[None])


def split3(x):
    h = x.astype(bf16).astype(f32)
    r = x - h
    m = r.astype(bf16).astype(f32)
    return h, m, r - m


def stack_a(x):
    h, m, l = split3(x)
    return jnp.concatenate([h, h, m, m, h, l], 0).astype(bf16)


def stack_b(x):
    h, m, l = split3(x)
    return jnp.concatenate([h, m, h, m, l, h], 0).astype(bf16)


def norm_sq(x):
    return x[0:1] * x[0:1] + x[1:2] * x[1:2] + x[2:3] * x[2:3]


def partner_tile(st):
    x, m, s = st[0:3], st[3:4], st[4:5]
    one = jnp.ones_like(m)
    rows = jnp.concatenate([x, norm_sq(x), jnp.log2(m), 0.5 * s * s, one, jnp.zeros_like(one)], 0)
    return stack_a(rows).T


def fill_partners(src, a_ref, at, count):
    step = min(16, count)

    def body(i, _):
        for u in range(step):
            b = i * step + u
            a_ref[at + b] = partner_tile(src[0:5, lanes(b)])
        return 0

    lax.fori_loop(0, count // step, body, 0)


def depth_table(iz, cz, fz):
    lo = cz.astype(i16)
    hi = ((cz + 1) & (MZ - 1)).astype(i16)
    w1 = fz.astype(bf16)
    w0 = (1.0 - fz).astype(bf16)
    return jnp.where(iz == lo, w0, jnp.where(iz == hi, w1, jnp.zeros_like(w1)))


def row_table(iy, cy, mx, fy):
    lo = (mx * (1.0 - fy)).astype(bf16)
    hi = (mx * fy).astype(bf16)
    zero = jnp.zeros_like(hi)
    main = jnp.where(iy == cy.astype(i16), lo, jnp.where(iy == (cy + 1).astype(i16), hi, zero))
    return main, jnp.where(cy.astype(i16) == MYD - 1, hi, zero)


def cell_rows(st, at, span):
    s = st[:, pl.ds(pl.multiple_of(at, BLK), span)]
    return s[3:4], s[5:6].astype(i32), s[6:7].astype(i32), s[7:8], s[8:9], s[9:10]


def deposit_own_kernel(st, pb, pc, grid, rim, a_own, lst, total):
    n = st.shape[1]
    half = n // 2
    nb = pc.shape[1]
    fill_partners(st, a_own, 0, nb)
    iz = lax.broadcasted_iota(i16, (MZ, SPAN), 0)
    iy = lax.broadcasted_iota(i16, (MYD, SPAN), 0)
    ir = lax.broadcasted_iota(i16, (16, SPAN), 0)
    zero = jnp.zeros((16, SPAN), bf16)

    def listed(b, pos):
        for k in range(NP):
            lst[pos + k] = pb[k, b] + b * 256
        return pos + pc[0, b]

    count = lax.fori_loop(0, nb, listed, i32(0), unroll=8)
    for k in range(GROUP):
        lst[count + k] = i32(nb * 256)
    total[0] = (count + GROUP - 1) // GROUP
    grid[...] = jnp.zeros_like(grid)
    rim[...] = jnp.zeros_like(rim)

    def first(i, _):
        m, cy, cz, fx, fy, fz = cell_rows(st, i * SPAN, SPAN)
        main0, edge0 = row_table(iy, cy, m * (1.0 - fx), fy)
        main1, edge1 = row_table(iy, cy, m * fx, fy)
        edge = jnp.where(ir == 0, edge0, jnp.where(ir == 1, edge1, zero))
        u = lax.dot_general(
            jnp.concatenate([main0, main1, edge], 0), depth_table(iz, cz, fz), NT, preferred_element_type=f32
        )
        grid[0] += u[0:MYD]
        grid[1] += u[MYD : 2 * MYD]
        rim[...] += u[2 * MYD : 2 * MYD + 8]
        return 0

    lax.fori_loop(0, half // SPAN, first, 0)

    def second(i, _):
        m, cy, cz, fx, fy, fz = cell_rows(st, half + i * SPAN, SPAN)
        main, edge = row_table(iy, cy, m * (1.0 - fx), fy)
        u = lax.dot_general(
            jnp.concatenate([main, jnp.where(ir == 1, edge, zero)], 0),
            depth_table(iz, cz, fz),
            NT,
            preferred_element_type=f32,
        )
        grid[1] += u[0:MYD]
        rim[...] += u[MYD : MYD + 8]
        return 0

    lax.fori_loop(0, half // SPAN, second, 0)


def deposit_own(st, pb, pc):
    nb = pc.shape[1]
    return pl.pallas_call(
        deposit_own_kernel,
        out_shape=[
            jax.ShapeDtypeStruct((XP, MYD, MZ), f32),
            jax.ShapeDtypeStruct((8, MZ), f32),
            jax.ShapeDtypeStruct((nb, BLK, KF), bf16),
            jax.ShapeDtypeStruct((nb * NP + NP + 2 * GROUP,), i32),
            jax.ShapeDtypeStruct((1,), i32),
        ],
        in_specs=[VM, SM, SM],
        out_specs=[VM, VM, VM, SM, SM],
        compiler_params=pltpu.CompilerParams(vmem_limit_bytes=16 << 20),
        cost_estimate=pl.CostEstimate(flops=4 * st.shape[1] * MYD * MZ, bytes_accessed=4 << 20, transcendentals=0),
        name="deposit_own",
    )(st, pb, pc)


def deposit_in_kernel(st, g_in, r_in, after, grid, rim, edge_row):
    n = st.shape[1]
    iz = lax.broadcasted_iota(i16, (MZ, SPAN), 0)
    iy = lax.broadcasted_iota(i16, (MYD, SPAN), 0)
    ir = lax.broadcasted_iota(i16, (16, SPAN), 0)
    zero = jnp.zeros((16, SPAN), bf16)
    grid[...] = g_in[...]
    rim[...] = r_in[...]

    def body(i, _):
        m, cy, cz, fx, fy, fz = cell_rows(st, i * SPAN, SPAN)
        main, edge = row_table(iy, cy, m * fx, fy)
        u = lax.dot_general(
            jnp.concatenate([main, jnp.where(ir == 0, edge, zero)], 0),
            depth_table(iz, cz, fz),
            NT,
            preferred_element_type=f32,
        )
        grid[0] += u[0:MYD]
        rim[...] += u[MYD : MYD + 8]
        return 0

    lax.fori_loop(0, n // SPAN, body, 0)
    edge_row[...] = grid[:, 0:1, :]


def deposit_in(st, g, r, after):
    return pl.pallas_call(
        deposit_in_kernel,
        out_shape=[
            jax.ShapeDtypeStruct((XP, MYD, MZ), f32),
            jax.ShapeDtypeStruct((8, MZ), f32),
            jax.ShapeDtypeStruct((XP, 1, MZ), f32),
        ],
        in_specs=[VM, VM, VM, AN],
        out_specs=[VM] * 3,
        compiler_params=pltpu.CompilerParams(vmem_limit_bytes=16 << 20),
        cost_estimate=pl.CostEstimate(flops=2 * st.shape[1] * MYD * MZ, bytes_accessed=4 << 20, transcendentals=0),
        name="deposit_in",
    )(st, g, r, after)


def density_kernel(own, lo, hi, a_own, lst, total, den, term, a_ref, b_ref, acc):
    nb = den.shape[0]
    hb = nb // 2
    fill_partners(lo, a_ref, 0, hb)
    fill_partners(hi, a_ref, hb + nb, hb)
    a_ref[hb : hb + nb] = a_own[...]

    def own_tile(i, _):
        st = own[0:5, lanes(i)]
        x, s = st[0:3], st[4:5]
        one = jnp.ones_like(s)
        zero = jnp.zeros_like(s)
        c = LOG2E / (s * s)
        b_ref[i] = stack_b(jnp.concatenate([2.0 * c * x, -c, one, zero, -c * norm_sq(x), zero], 0))
        return 0

    lax.fori_loop(0, nb, own_tile, 0, unroll=4)
    b_ref[nb] = jnp.zeros((KF, BLK), bf16)
    acc[...] = jnp.zeros_like(acc)

    def main(it, _):
        for g in range(GROUP):
            code = lst[it * GROUP + g]
            e = jnp.dot(a_ref[code & 255], b_ref[code >> 8], preferred_element_type=f32)
            acc[code >> 8] += jnp.exp2(e).reshape(BLK // 8, 8, BLK).sum(0)
        return 0

    lax.fori_loop(0, total[0], main, 0)
    d = acc[0:nb].sum(1) * (1.0 / (NP * BLK))
    den[...] = d
    term[...] = jnp.exp2(jnp.log2(d) * (-1.0 / 3.0))


def density(own, lo, hi, a_own, lst, total):
    nb = a_own.shape[0]
    return pl.pallas_call(
        density_kernel,
        out_shape=[
            jax.ShapeDtypeStruct((nb, BLK), f32),
            jax.ShapeDtypeStruct((nb, BLK), f32),
            jax.ShapeDtypeStruct((2 * nb, BLK, KF), bf16),
        ],
        in_specs=[VM, VM, VM, VM, SM, SM],
        out_specs=[VM] * 3,
        scratch_shapes=[pltpu.VMEM((nb + 1, KF, BLK), bf16), pltpu.VMEM((nb + 1, 8, BLK), f32)],
        compiler_params=pltpu.CompilerParams(vmem_limit_bytes=16 << 20),
        cost_estimate=pl.CostEstimate(flops=12 * nb * NP * BLK * BLK, bytes_accessed=8 << 20, transcendentals=nb * NP * BLK * BLK),
        name="density",
    )(own, lo, hi, a_own, lst, total)


def force_kernel(own, lo, hi, a_ref, town, tlo, thi, lst, total, out, b_ref, v_ref, acc):
    nb = town.shape[0]
    hb = nb // 2

    def sources(src, t, at, count):
        def body(i, _):
            st = src[0:5, lanes(i)]
            x, m = st[0:3], st[3:4]
            mt = m * t[pl.ds(i, 1), :]
            v = jnp.concatenate([m, m * x, mt, mt * x], 0)
            h = v.astype(bf16).astype(f32)
            v_ref[at + i] = jnp.concatenate([h, v - h], 0).astype(bf16)
            return 0

        lax.fori_loop(0, count, body, 0, unroll=8)

    sources(lo, tlo, 0, hb)
    sources(own, town, hb, nb)
    sources(hi, thi, hb + nb, hb)

    def own_tile(i, _):
        st = own[0:5, lanes(i)]
        x, s = st[0:3], st[4:5]
        one = jnp.ones_like(s)
        z = jnp.zeros_like(s)
        dist = jnp.concatenate([(2.0 * LOG2E) * x, -LOG2E * one, z, z, -LOG2E * norm_sq(x), z], 0)
        spread = jnp.concatenate([z, z, z, z, z, one, 0.5 * s * s, z], 0)
        b_ref[i, :, 0:BLK] = stack_b(dist)
        b_ref[i, :, BLK : 2 * BLK] = stack_b(spread)
        return 0

    lax.fori_loop(0, nb, own_tile, 0, unroll=4)
    b_ref[nb] = jnp.ones((KF, 2 * BLK), bf16)
    acc[...] = jnp.zeros_like(acc)
    lag = 8

    def main(it, _):
        codes = [lst[it * GROUP + g] for g in range(GROUP)]
        forms = {}
        weights = {}
        for step in range(GROUP + 2 * lag):
            if step < GROUP:
                code = codes[step]
                forms[step] = jnp.dot(a_ref[code & 255], b_ref[code >> 8], preferred_element_type=f32)
            g = step - lag
            if 0 <= g < GROUP:
                e = forms.pop(g)
                r = pl.reciprocal(e[:, BLK : 2 * BLK], approx=True)
                weights[g] = (jnp.exp2(e[:, 0:BLK] * r) * r).astype(bf16)
            g = step - 2 * lag
            if 0 <= g < GROUP:
                code = codes[g]
                acc[code >> 8] += jnp.dot(v_ref[code & 255], weights.pop(g), preferred_element_type=f32)
        return 0

    lax.fori_loop(0, total[0], main, 0)

    def finish(i, _):
        a = acc[i]
        s = a[0:8] + a[8:16]
        x = own[0:3, lanes(i)]
        t = town[pl.ds(i, 1), :]
        f = t * (x * s[0:1] - s[1:4]) + (x * s[4:5] - s[5:8])
        out[:, lanes(i)] = f * (2.0 / (NP * BLK))
        return 0

    lax.fori_loop(0, nb, finish, 0, unroll=8)


def force(own, lo, hi, a, town, tlo, thi, lst, total):
    nb = town.shape[0]
    return pl.pallas_call(
        force_kernel,
        out_shape=jax.ShapeDtypeStruct((3, nb * BLK), f32),
        in_specs=[VM] * 7 + [SM, SM],
        out_specs=VM,
        scratch_shapes=[
            pltpu.VMEM((nb + 1, KF, 2 * BLK), bf16),
            pltpu.VMEM((2 * nb, 16, BLK), bf16),
            pltpu.VMEM((nb + 1, 16, BLK), f32),
        ],
        compiler_params=pltpu.CompilerParams(vmem_limit_bytes=16 << 20),
        cost_estimate=pl.CostEstimate(flops=24 * nb * NP * BLK * BLK, bytes_accessed=8 << 20, transcendentals=2 * nb * NP * BLK * BLK),
        name="force",
    )(own, lo, hi, a, town, tlo, thi, lst, total)


def on_device(positions, mass, smooth, cell_y, cell_z, cic_frac, pair_blocks, pair_count):
    hb = pair_blocks.shape[0] // 2
    slabs = lax.axis_size("slab")
    cols = lax.axis_size("col")
    up = [(i, (i + 1) % slabs) for i in range(slabs)]
    down = [((i + 1) % slabs, i) for i in range(slabs)]
    right = [(i, (i + 1) % cols) for i in range(cols)]
    own, tail, head, pairs, counts = pack(
        positions, mass, smooth, cell_y, cell_z, cic_frac, pair_blocks.T, pair_count
    )
    lo = lax.ppermute(tail, "slab", up)
    hi = lax.ppermute(head, "slab", down)
    grid, rim, a_own, lst, total = deposit_own(own, pairs, counts)
    den, term, a = density(own, lo, hi, a_own, lst, total)
    tlo = lax.ppermute(term[hb:], "slab", up)
    thi = lax.ppermute(term[:hb], "slab", down)
    grid, rim, edge_row = deposit_in(lo, grid, rim, term)
    rows = lax.ppermute(rim[:XP], "col", right)
    acceleration = force(own, lo, hi, a, term, tlo, thi, lst, total)
    rows, acceleration = lax.optimization_barrier((rows, acceleration))
    grid = lax.dynamic_update_slice(grid, edge_row + rows[:, None], (0, 0, 0))
    return den.reshape(-1), acceleration, grid


def solution(mesh):
    return jax.shard_map(
        on_device,
        mesh=mesh,
        in_specs=(
            P(None, ("slab", "col")),
            P(("slab", "col")),
            P(("slab", "col")),
            P(("slab", "col")),
            P(("slab", "col")),
            P(None, ("slab", "col")),
            P(("slab", "col"), None),
            P(("slab", "col")),
        ),
        out_specs=(P(("slab", "col")), P(None, ("slab", "col")), P("slab", "col", None)),
        check_vma=False,
    )
```

```python
import functools

import jax
import jax.numpy as jnp
from jax import lax
from jax.experimental import pallas as pl
from jax.experimental.pallas import tpu as pltpu
from jax.sharding import PartitionSpec as P

BLK = 128
NP = 9
XP = 2
MYD = 128
MZ = 1024
LOG2E = 1.4426950408889634
KF = 48
GROUP = 32
SPAN = 1024
ZB = 512

f32 = jnp.float32
bf16 = jnp.bfloat16
i16 = jnp.int16
i32 = jnp.int32

VM = pl.BlockSpec(memory_space=pltpu.VMEM)
SM = pl.BlockSpec(memory_space=pltpu.SMEM)
AN = pl.BlockSpec(memory_space=pl.ANY)
HB = pl.BlockSpec(memory_space=pltpu.HBM)
NT = (((1,), (1,)), ((), ()))


def lanes(i, width=BLK):
    return pl.ds(pl.multiple_of(i * width, BLK), width)


def pack_kernel(pos, mass, smooth, cy, cz, frac, pairs, counts, own, tail, head, lst, spairs, scounts, vpos, vmass, vsmooth, vcy, vcz, vfrac, sems):
    half = own.shape[1] // 2
    moves = (
        (pos, vpos),
        (mass, vmass),
        (smooth, vsmooth),
        (cy, vcy),
        (cz, vcz),
        (frac, vfrac),
        (pairs, spairs),
        (counts, scounts),
    )
    copies = [pltpu.make_async_copy(src, dst, sems.at[k]) for k, (src, dst) in enumerate(moves)]
    for copy in copies:
        copy.start()
    for copy in copies[-2:] + copies[:-2]:
        copy.wait()
    nb = counts.shape[1]
    at = i32(0)
    for b in range(nb):
        for k in range(NP):
            lst[at + k] = spairs[k, b] + b * 256
        at = at + scounts[0, b]
    for k in range(GROUP):
        lst[at + k] = i32(nb * 256)
    lst[lst.shape[0] - 1] = (at + GROUP - 1) // GROUP
    own[0:3] = vpos[...]
    own[3:4] = vmass[...]
    own[4:5] = vsmooth[...]
    own[5:6] = vcy[...].astype(f32)
    own[6:7] = vcz[...].astype(f32)
    own[7:10] = vfrac[...]
    tail[...] = own[:, half:]
    head[...] = own[0:5, :half]


def pack(positions, mass, smooth, cell_y, cell_z, cic_frac, pairs, counts):
    n = mass.shape[0]
    nb = counts.shape[0]
    return pl.pallas_call(
        pack_kernel,
        out_shape=[
            jax.ShapeDtypeStruct((10, n), f32),
            jax.ShapeDtypeStruct((10, n // 2), f32),
            jax.ShapeDtypeStruct((5, n // 2), f32),
            jax.ShapeDtypeStruct((nb * NP + NP + 2 * GROUP,), i32),
        ],
        in_specs=[HB] * 8,
        out_specs=[VM] * 3 + [SM],
        scratch_shapes=[
            pltpu.SMEM((NP, nb), i32),
            pltpu.SMEM((1, nb), i32),
            pltpu.VMEM((3, n), f32),
            pltpu.VMEM((1, n), f32),
            pltpu.VMEM((1, n), f32),
            pltpu.VMEM((1, n), i32),
            pltpu.VMEM((1, n), i32),
            pltpu.VMEM((3, n), f32),
            pltpu.SemaphoreType.DMA((8,)),
        ],
        name="pack",
    )(positions, mass[None], smooth[None], cell_y[None], cell_z[None], cic_frac, pairs, counts[None])


def split3(x):
    h = x.astype(bf16).astype(f32)
    r = x - h
    m = r.astype(bf16).astype(f32)
    return h, m, r - m


def stack_a(x):
    h, m, l = split3(x)
    return jnp.concatenate([h, h, m, m, h, l], 0).astype(bf16)


def stack_b(x):
    h, m, l = split3(x)
    return jnp.concatenate([h, m, h, m, l, h], 0).astype(bf16)


def norm_sq(x):
    return x[0:1] * x[0:1] + x[1:2] * x[1:2] + x[2:3] * x[2:3]


def partner_tile(st):
    x, m, s = st[0:3], st[3:4], st[4:5]
    one = jnp.ones_like(m)
    rows = jnp.concatenate([x, norm_sq(x), jnp.log2(m), 0.5 * s * s, one, jnp.zeros_like(one)], 0)
    return stack_a(rows).T


def fill_partners(src, a_ref, at, count):
    step = min(16, count)

    def body(i, _):
        for u in range(step):
            b = i * step + u
            a_ref[at + b] = partner_tile(src[0:5, lanes(b)])
        return 0

    lax.fori_loop(0, count // step, body, 0)


def hat_parts(c, low, high, wrap):
    odd = (c & 1) != 0
    row = lax.broadcasted_iota(i32, (16, c.shape[1]), 0)
    even_row = (row & 1) == 0
    at = jnp.where(even_row, ((c + 1) >> 1) & wrap, c >> 1)
    value = jnp.where(even_row, jnp.where(odd, high, low), jnp.where(odd, low, high))
    hit = jnp.where((at & 7) == (row >> 1), value, 0.0)
    return (at >> 3).astype(f32), hit.astype(bf16)


def hat_table(top, hit, tiles):
    zero = jnp.zeros_like(hit)
    return jnp.concatenate([jnp.where(top == jnp.full((), t, bf16), hit, zero) for t in range(tiles)], 0)


def row_table(cy, mx, fy):
    high = mx * fy
    top, hit = hat_parts(cy, mx * (1.0 - fy), high, MYD - 1)
    edge = jnp.where(cy == MYD - 1, high, 0.0).astype(bf16)
    return hat_table(top.astype(bf16), hit, MYD // 16), edge


def fill_tables(st, at, k, planes, edges, rows_ref, top_ref, hit_ref):
    span = pl.ds(k * SPAN, SPAN)
    s = st[:, pl.ds(at + k * SPAN, SPAN)]
    m, cy, cz, fx, fy, fz = s[3:4], s[5:6].astype(i32), s[6:7].astype(i32), s[7:8], s[8:9], s[9:10]
    row = lax.broadcasted_iota(i32, (16, SPAN), 0)
    rim = jnp.zeros((16, SPAN), bf16)
    for n, (plane, edge_at) in enumerate(zip(planes, edges)):
        main, edge = row_table(cy, m * (fx if plane else 1.0 - fx), fy)
        rows_ref[n * MYD : (n + 1) * MYD, span] = main
        rim = jnp.where(row == edge_at, edge.astype(f32), rim.astype(f32)).astype(bf16)
    rows_ref[len(planes) * MYD : len(planes) * MYD + 16, span] = rim
    top, hit = hat_parts(cz, 1.0 - fz, fz, MZ // 2 - 1)
    top_ref[:, span] = top
    hit_ref[:, span] = hit


def table_scratch(planes, n):
    return [
        pltpu.VMEM((planes * MYD + 16, n), bf16),
        pltpu.VMEM((16, n), f32),
        pltpu.VMEM((16, n), bf16),
    ]


def deposit_dot(z, rows_ref, top_ref, hit_ref):
    tiles = ZB // 16
    top = (top_ref[...] - (z * tiles).astype(f32)).astype(bf16)
    return lax.dot_general(rows_ref[...], hat_table(top, hit_ref[...], tiles), NT, preferred_element_type=f32)


def deposit_own_kernel(st, grid, rim, a_own, rows1, top1, hit1, rows2, top2, hit2):
    n = st.shape[1]
    half = n // 2
    fill_partners(st, a_own, 0, a_own.shape[0])
    for k in range(half // SPAN):
        fill_tables(st, 0, k, (0, 1), (0, 1), rows1, top1, hit1)
        fill_tables(st, half, k, (0,), (1,), rows2, top2, hit2)

    def body(z, _):
        at = lanes(z, ZB)
        u = deposit_dot(z, rows1, top1, hit1)
        v = deposit_dot(z, rows2, top2, hit2)
        grid[0, :, at] = u[0:MYD]
        grid[1, :, at] = u[MYD : 2 * MYD] + v[0:MYD]
        rim[:, at] = u[2 * MYD : 2 * MYD + 8] + v[MYD : MYD + 8]
        return 0

    lax.fori_loop(0, MZ // ZB, body, 0)


def deposit_own(st):
    nb = st.shape[1] // BLK
    return pl.pallas_call(
        deposit_own_kernel,
        out_shape=[
            jax.ShapeDtypeStruct((XP, MYD, MZ), f32),
            jax.ShapeDtypeStruct((8, MZ), f32),
            jax.ShapeDtypeStruct((nb, BLK, KF), bf16),
        ],
        in_specs=[VM],
        out_specs=[VM] * 3,
        scratch_shapes=table_scratch(2, st.shape[1] // 2) + table_scratch(1, st.shape[1] // 2),
        compiler_params=pltpu.CompilerParams(vmem_limit_bytes=16 << 20),
        cost_estimate=pl.CostEstimate(flops=4 * st.shape[1] * MYD * MZ, bytes_accessed=4 << 20, transcendentals=0),
        name="deposit_own",
    )(st)


def deposit_in_kernel(st, g_in, r_in, after, grid, rim, edge_row, rows, top, hit):
    for k in range(st.shape[1] // SPAN):
        fill_tables(st, 0, k, (1,), (0,), rows, top, hit)

    def body(z, _):
        at = lanes(z, ZB)
        u = deposit_dot(z, rows, top, hit)
        grid[0, :, at] = g_in[0, :, at] + u[0:MYD]
        grid[1, :, at] = g_in[1, :, at]
        rim[:, at] = r_in[:, at] + u[MYD : MYD + 8]
        return 0

    lax.fori_loop(0, MZ // ZB, body, 0)
    edge_row[...] = grid[:, 0:1, :]


def deposit_in(st, g, r, after):
    return pl.pallas_call(
        deposit_in_kernel,
        out_shape=[
            jax.ShapeDtypeStruct((XP, MYD, MZ), f32),
            jax.ShapeDtypeStruct((8, MZ), f32),
            jax.ShapeDtypeStruct((XP, 1, MZ), f32),
        ],
        in_specs=[VM, VM, VM, AN],
        out_specs=[VM] * 3,
        scratch_shapes=table_scratch(1, st.shape[1]),
        compiler_params=pltpu.CompilerParams(vmem_limit_bytes=16 << 20),
        cost_estimate=pl.CostEstimate(flops=2 * st.shape[1] * MYD * MZ, bytes_accessed=4 << 20, transcendentals=0),
        name="deposit_in",
    )(st, g, r, after)


def density_kernel(own, lo, hi, a_own, listed, den, term, a_ref, b_ref, acc, lst, sem):
    nb = den.shape[0]
    hb = nb // 2
    fetch = pltpu.make_async_copy(listed, lst, sem)
    fetch.start()
    fill_partners(lo, a_ref, 0, hb)
    fill_partners(hi, a_ref, hb + nb, hb)
    a_ref[hb : hb + nb] = a_own[...]

    def own_tile(i, _):
        st = own[0:5, lanes(i)]
        x, s = st[0:3], st[4:5]
        one = jnp.ones_like(s)
        zero = jnp.zeros_like(s)
        c = LOG2E / (s * s)
        b_ref[i] = stack_b(jnp.concatenate([2.0 * c * x, -c, one, zero, -c * norm_sq(x), zero], 0))
        return 0

    lax.fori_loop(0, nb, own_tile, 0, unroll=4)
    b_ref[nb] = jnp.zeros((KF, BLK), bf16)
    acc[...] = jnp.zeros_like(acc)

    def main(it, _):
        for g in range(GROUP):
            code = lst[it * GROUP + g]
            e = jnp.dot(a_ref[code & 255], b_ref[code >> 8], preferred_element_type=f32)
            acc[code >> 8] += jnp.exp2(e).reshape(BLK // 8, 8, BLK).sum(0)
        return 0

    fetch.wait()
    lax.fori_loop(0, lst[lst.shape[0] - 1], main, 0)
    d = acc[0:nb].sum(1) * (1.0 / (NP * BLK))
    den[...] = d
    term[...] = jnp.exp2(jnp.log2(d) * (-1.0 / 3.0))


def density(own, lo, hi, a_own, lst):
    nb = a_own.shape[0]
    return pl.pallas_call(
        density_kernel,
        out_shape=[
            jax.ShapeDtypeStruct((nb, BLK), f32),
            jax.ShapeDtypeStruct((nb, BLK), f32),
            jax.ShapeDtypeStruct((2 * nb, BLK, KF), bf16),
        ],
        in_specs=[VM, VM, VM, VM, AN],
        out_specs=[VM] * 3,
        scratch_shapes=[
            pltpu.VMEM((nb + 1, KF, BLK), bf16),
            pltpu.VMEM((nb + 1, 8, BLK), f32),
            pltpu.SMEM(lst.shape, i32),
            pltpu.SemaphoreType.DMA(()),
        ],
        compiler_params=pltpu.CompilerParams(vmem_limit_bytes=16 << 20),
        cost_estimate=pl.CostEstimate(flops=12 * nb * NP * BLK * BLK, bytes_accessed=8 << 20, transcendentals=nb * NP * BLK * BLK),
        name="density",
    )(own, lo, hi, a_own, lst)


def force_kernel(own, lo, hi, a_ref, town, tlo, thi, listed, out, b_ref, v_ref, acc, lst, sem):
    nb = town.shape[0]
    hb = nb // 2
    fetch = pltpu.make_async_copy(listed, lst, sem)
    fetch.start()

    def sources(src, t, at, count):
        def body(i, _):
            st = src[0:5, lanes(i)]
            x, m = st[0:3], st[3:4]
            mt = m * t[pl.ds(i, 1), :]
            v = jnp.concatenate([m, m * x, mt, mt * x], 0)
            h = v.astype(bf16).astype(f32)
            v_ref[at + i] = jnp.concatenate([h, v - h], 0).astype(bf16)
            return 0

        lax.fori_loop(0, count, body, 0, unroll=8)

    sources(lo, tlo, 0, hb)
    sources(own, town, hb, nb)
    sources(hi, thi, hb + nb, hb)

    def own_tile(i, _):
        st = own[0:5, lanes(i)]
        x, s = st[0:3], st[4:5]
        one = jnp.ones_like(s)
        z = jnp.zeros_like(s)
        dist = jnp.concatenate([(2.0 * LOG2E) * x, -LOG2E * one, z, z, -LOG2E * norm_sq(x), z], 0)
        spread = jnp.concatenate([z, z, z, z, z, one, 0.5 * s * s, z], 0)
        b_ref[i, :, 0:BLK] = stack_b(dist)
        b_ref[i, :, BLK : 2 * BLK] = stack_b(spread)
        return 0

    lax.fori_loop(0, nb, own_tile, 0, unroll=4)
    b_ref[nb] = jnp.ones((KF, 2 * BLK), bf16)
    acc[...] = jnp.zeros_like(acc)
    lag = 8

    def main(it, _):
        codes = [lst[it * GROUP + g] for g in range(GROUP)]
        forms = {}
        weights = {}
        for step in range(GROUP + 2 * lag):
            if step < GROUP:
                code = codes[step]
                forms[step] = jnp.dot(a_ref[code & 255], b_ref[code >> 8], preferred_element_type=f32)
            g = step - lag
            if 0 <= g < GROUP:
                e = forms.pop(g)
                r = pl.reciprocal(e[:, BLK : 2 * BLK], approx=True)
                weights[g] = (jnp.exp2(e[:, 0:BLK] * r) * r).astype(bf16)
            g = step - 2 * lag
            if 0 <= g < GROUP:
                code = codes[g]
                acc[code >> 8] += jnp.dot(v_ref[code & 255], weights.pop(g), preferred_element_type=f32)
        return 0

    fetch.wait()
    lax.fori_loop(0, lst[lst.shape[0] - 1], main, 0)

    def finish(i, _):
        a = acc[i]
        s = a[0:8] + a[8:16]
        x = own[0:3, lanes(i)]
        t = town[pl.ds(i, 1), :]
        f = t * (x * s[0:1] - s[1:4]) + (x * s[4:5] - s[5:8])
        out[:, lanes(i)] = f * (2.0 / (NP * BLK))
        return 0

    lax.fori_loop(0, nb, finish, 0, unroll=8)


def force(own, lo, hi, a, town, tlo, thi, lst):
    nb = town.shape[0]
    return pl.pallas_call(
        force_kernel,
        out_shape=jax.ShapeDtypeStruct((3, nb * BLK), f32),
        in_specs=[VM] * 7 + [AN],
        out_specs=VM,
        scratch_shapes=[
            pltpu.VMEM((nb + 1, KF, 2 * BLK), bf16),
            pltpu.VMEM((2 * nb, 16, BLK), bf16),
            pltpu.VMEM((nb + 1, 16, BLK), f32),
            pltpu.SMEM(lst.shape, i32),
            pltpu.SemaphoreType.DMA(()),
        ],
        compiler_params=pltpu.CompilerParams(vmem_limit_bytes=16 << 20),
        cost_estimate=pl.CostEstimate(flops=24 * nb * NP * BLK * BLK, bytes_accessed=8 << 20, transcendentals=2 * nb * NP * BLK * BLK),
        name="force",
    )(own, lo, hi, a, town, tlo, thi, lst)


def on_device(positions, mass, smooth, cell_y, cell_z, cic_frac, pair_blocks, pair_count):
    hb = pair_blocks.shape[0] // 2
    slabs = lax.axis_size("slab")
    cols = lax.axis_size("col")
    up = [(i, (i + 1) % slabs) for i in range(slabs)]
    down = [((i + 1) % slabs, i) for i in range(slabs)]
    right = [(i, (i + 1) % cols) for i in range(cols)]
    own, tail, head, lst = pack(
        positions, mass, smooth, cell_y, cell_z, cic_frac, pair_blocks.T, pair_count
    )
    lo = lax.ppermute(tail, "slab", up)
    hi = lax.ppermute(head, "slab", down)
    grid, rim, a_own = deposit_own(own)
    den, term, a = density(own, lo, hi, a_own, lst)
    tlo = lax.ppermute(term[hb:], "slab", up)
    thi = lax.ppermute(term[:hb], "slab", down)
    grid, rim, edge_row = deposit_in(lo, grid, rim, term)
    rows = lax.ppermute(rim[:XP], "col", right)
    acceleration = force(own, lo, hi, a, term, tlo, thi, lst)
    rows, acceleration = lax.optimization_barrier((rows, acceleration))
    grid = lax.dynamic_update_slice(grid, edge_row + rows[:, None], (0, 0, 0))
    return den.reshape(-1), acceleration, grid


def solution(mesh):
    return jax.shard_map(
        on_device,
        mesh=mesh,
        in_specs=(
            P(None, ("slab", "col")),
            P(("slab", "col")),
            P(("slab", "col")),
            P(("slab", "col")),
            P(("slab", "col")),
            P(None, ("slab", "col")),
            P(("slab", "col"), None),
            P(("slab", "col")),
        ),
        out_specs=(P(("slab", "col")), P(None, ("slab", "col")), P("slab", "col", None)),
        check_vma=False,
    )
```

```python
import functools

import jax
import jax.numpy as jnp
from jax import lax
from jax.experimental import pallas as pl
from jax.experimental.pallas import tpu as pltpu
from jax.sharding import PartitionSpec as P

BLK = 128
NP = 9
XP = 2
MYD = 128
MZ = 1024
LOG2E = 1.4426950408889634
KF = 48
GROUP = 64
REST = 16
SPAN = 1024
ZB = 1024

f32 = jnp.float32
bf16 = jnp.bfloat16
i16 = jnp.int16
i32 = jnp.int32

VM = pl.BlockSpec(memory_space=pltpu.VMEM)
SM = pl.BlockSpec(memory_space=pltpu.SMEM)
AN = pl.BlockSpec(memory_space=pl.ANY)
HB = pl.BlockSpec(memory_space=pltpu.HBM)
NT = (((1,), (1,)), ((), ()))


def lanes(i, width=BLK):
    return pl.ds(pl.multiple_of(i * width, BLK), width)


def pack_kernel(pos, mass, smooth, cy, cz, frac, pairs, counts, own, tail, head, lst, spairs, scounts, vpos, vmass, vsmooth, vcy, vcz, vfrac, sems):
    half = own.shape[1] // 2
    moves = (
        (pos, vpos),
        (mass, vmass),
        (smooth, vsmooth),
        (cy, vcy),
        (cz, vcz),
        (frac, vfrac),
        (pairs, spairs),
        (counts, scounts),
    )
    copies = [pltpu.make_async_copy(src, dst, sems.at[k]) for k, (src, dst) in enumerate(moves)]
    for copy in copies:
        copy.start()
    for copy in copies[-2:] + copies[:-2]:
        copy.wait()
    nb = counts.shape[1]
    at = i32(0)
    for b in range(nb):
        for k in range(NP):
            lst[at + k] = spairs[k, b] + b * 256
        at = at + scounts[0, b]
    for k in range(REST):
        lst[at + k] = i32(nb * 256)
    lst[lst.shape[0] - 1] = at
    own[0:3] = vpos[...]
    own[3:4] = vmass[...]
    own[4:5] = vsmooth[...]
    own[5:6] = vcy[...].astype(f32)
    own[6:7] = vcz[...].astype(f32)
    own[7:10] = vfrac[...]
    tail[...] = own[:, half:]
    head[...] = own[0:5, :half]


def pack(positions, mass, smooth, cell_y, cell_z, cic_frac, pairs, counts):
    n = mass.shape[0]
    nb = counts.shape[0]
    return pl.pallas_call(
        pack_kernel,
        out_shape=[
            jax.ShapeDtypeStruct((10, n), f32),
            jax.ShapeDtypeStruct((10, n // 2), f32),
            jax.ShapeDtypeStruct((5, n // 2), f32),
            jax.ShapeDtypeStruct((nb * NP + NP + 2 * REST,), i32),
        ],
        in_specs=[HB] * 8,
        out_specs=[VM] * 3 + [SM],
        scratch_shapes=[
            pltpu.SMEM((NP, nb), i32),
            pltpu.SMEM((1, nb), i32),
            pltpu.VMEM((3, n), f32),
            pltpu.VMEM((1, n), f32),
            pltpu.VMEM((1, n), f32),
            pltpu.VMEM((1, n), i32),
            pltpu.VMEM((1, n), i32),
            pltpu.VMEM((3, n), f32),
            pltpu.SemaphoreType.DMA((8,)),
        ],
        name="pack",
    )(positions, mass[None], smooth[None], cell_y[None], cell_z[None], cic_frac, pairs, counts[None])


def split3(x):
    h = x.astype(bf16).astype(f32)
    r = x - h
    m = r.astype(bf16).astype(f32)
    return h, m, r - m


def stack_a(x):
    h, m, l = split3(x)
    return jnp.concatenate([h, h, m, m, h, l], 0).astype(bf16)


def stack_b(x):
    h, m, l = split3(x)
    return jnp.concatenate([h, m, h, m, l, h], 0).astype(bf16)


def norm_sq(x):
    return x[0:1] * x[0:1] + x[1:2] * x[1:2] + x[2:3] * x[2:3]


def partner_tile(st):
    x, m, s = st[0:3], st[3:4], st[4:5]
    one = jnp.ones_like(m)
    rows = jnp.concatenate([x, norm_sq(x), jnp.log2(m), 0.5 * s * s, one, jnp.zeros_like(one)], 0)
    return stack_a(rows).T


def fill_partners(src, a_ref, at, count):
    step = min(16, count)

    def body(i, _):
        for u in range(step):
            b = i * step + u
            a_ref[at + b] = partner_tile(src[0:5, lanes(b)])
        return 0

    lax.fori_loop(0, count // step, body, 0)


def hat_parts(c, low, high, wrap):
    odd = (c & 1) != 0
    row = lax.broadcasted_iota(i32, (16, c.shape[1]), 0)
    even_row = (row & 1) == 0
    at = jnp.where(even_row, ((c + 1) >> 1) & wrap, c >> 1)
    value = jnp.where(even_row, jnp.where(odd, high, low), jnp.where(odd, low, high))
    hit = jnp.where((at & 7) == (row >> 1), value, 0.0)
    return (at >> 3).astype(f32), hit.astype(bf16)


def hat_table(top, hit, tiles):
    zero = jnp.zeros_like(hit)
    return jnp.concatenate([jnp.where(top == jnp.full((), t, bf16), hit, zero) for t in range(tiles)], 0)


def row_table(cy, mx, fy):
    high = mx * fy
    top, hit = hat_parts(cy, mx * (1.0 - fy), high, MYD - 1)
    edge = jnp.where(cy == MYD - 1, high, 0.0).astype(bf16)
    return hat_table(top.astype(bf16), hit, MYD // 16), edge


def fill_tables(st, at, k, planes, edges, rows_ref, top_ref, hit_ref):
    span = pl.ds(k * SPAN, SPAN)
    s = st[:, pl.ds(at + k * SPAN, SPAN)]
    m, cy, cz, fx, fy, fz = s[3:4], s[5:6].astype(i32), s[6:7].astype(i32), s[7:8], s[8:9], s[9:10]
    row = lax.broadcasted_iota(i32, (16, SPAN), 0)
    rim = jnp.zeros((16, SPAN), bf16)
    for n, (plane, edge_at) in enumerate(zip(planes, edges)):
        main, edge = row_table(cy, m * (fx if plane else 1.0 - fx), fy)
        rows_ref[n * MYD : (n + 1) * MYD, span] = main
        rim = jnp.where(row == edge_at, edge.astype(f32), rim.astype(f32)).astype(bf16)
    rows_ref[len(planes) * MYD : len(planes) * MYD + 16, span] = rim
    top, hit = hat_parts(cz, 1.0 - fz, fz, MZ // 2 - 1)
    top_ref[:, span] = top
    hit_ref[:, span] = hit


def table_scratch(planes, n):
    return [
        pltpu.VMEM((planes * MYD + 16, n), bf16),
        pltpu.VMEM((16, n), f32),
        pltpu.VMEM((16, n), bf16),
    ]


def deposit_dot(z, rows_ref, top_ref, hit_ref):
    tiles = ZB // 16
    top = (top_ref[...] - (z * tiles).astype(f32)).astype(bf16)
    return lax.dot_general(rows_ref[...], hat_table(top, hit_ref[...], tiles), NT, preferred_element_type=f32)


def deposit_dot_one(z, rows_ref, top_ref, hit_ref):
    tiles = ZB // 16
    top = (top_ref[...] - (z * tiles).astype(f32)).astype(bf16)
    u = lax.dot_general(hat_table(top, hit_ref[...], tiles), rows_ref[...], NT, preferred_element_type=f32)
    return u.T


def deposit_own_kernel(st, grid, rim, a_own, rows1, top1, hit1, rows2, top2, hit2):
    n = st.shape[1]
    half = n // 2
    fill_partners(st, a_own, 0, a_own.shape[0])
    for k in range(half // SPAN):
        fill_tables(st, 0, k, (0, 1), (0, 1), rows1, top1, hit1)
        fill_tables(st, half, k, (0,), (1,), rows2, top2, hit2)

    def body(z, _):
        at = lanes(z, ZB)
        u = deposit_dot(z, rows1, top1, hit1)
        v = deposit_dot_one(z, rows2, top2, hit2)
        grid[0, :, at] = u[0:MYD]
        grid[1, :, at] = u[MYD : 2 * MYD] + v[0:MYD]
        rim[:, at] = u[2 * MYD : 2 * MYD + 8] + v[MYD : MYD + 8]
        return 0

    lax.fori_loop(0, MZ // ZB, body, 0)


def deposit_own(st):
    nb = st.shape[1] // BLK
    return pl.pallas_call(
        deposit_own_kernel,
        out_shape=[
            jax.ShapeDtypeStruct((XP, MYD, MZ), f32),
            jax.ShapeDtypeStruct((8, MZ), f32),
            jax.ShapeDtypeStruct((nb, BLK, KF), bf16),
        ],
        in_specs=[VM],
        out_specs=[VM] * 3,
        scratch_shapes=table_scratch(2, st.shape[1] // 2) + table_scratch(1, st.shape[1] // 2),
        compiler_params=pltpu.CompilerParams(vmem_limit_bytes=16 << 20),
        cost_estimate=pl.CostEstimate(flops=4 * st.shape[1] * MYD * MZ, bytes_accessed=4 << 20, transcendentals=0),
        name="deposit_own",
    )(st)


def deposit_in_kernel(st, g_in, r_in, after, grid, rim, edge_row, rows, top, hit):
    for k in range(st.shape[1] // SPAN):
        fill_tables(st, 0, k, (1,), (0,), rows, top, hit)

    def body(z, _):
        at = lanes(z, ZB)
        u = deposit_dot_one(z, rows, top, hit)
        grid[0, :, at] = g_in[0, :, at] + u[0:MYD]
        grid[1, :, at] = g_in[1, :, at]
        rim[:, at] = r_in[:, at] + u[MYD : MYD + 8]
        return 0

    lax.fori_loop(0, MZ // ZB, body, 0)
    edge_row[...] = grid[:, 0:1, :]


def deposit_in(st, g, r, after):
    return pl.pallas_call(
        deposit_in_kernel,
        out_shape=[
            jax.ShapeDtypeStruct((XP, MYD, MZ), f32),
            jax.ShapeDtypeStruct((8, MZ), f32),
            jax.ShapeDtypeStruct((XP, 1, MZ), f32),
        ],
        in_specs=[VM, VM, VM, AN],
        out_specs=[VM] * 3,
        scratch_shapes=table_scratch(1, st.shape[1]),
        compiler_params=pltpu.CompilerParams(vmem_limit_bytes=16 << 20),
        cost_estimate=pl.CostEstimate(flops=2 * st.shape[1] * MYD * MZ, bytes_accessed=4 << 20, transcendentals=0),
        name="deposit_in",
    )(st, g, r, after)


def for_groups(lst, work):
    live = lst[lst.shape[0] - 1]
    full = live // GROUP

    def whole(it, _):
        work(it * GROUP, GROUP)
        return 0

    def rest(it, _):
        work(full * GROUP + it * REST, REST)
        return 0

    lax.fori_loop(0, full, whole, 0)
    lax.fori_loop(0, (live - full * GROUP + REST - 1) // REST, rest, 0)


def density_kernel(own, lo, hi, a_own, listed, den, term, a_ref, b_ref, acc, lst, sem):
    nb = den.shape[0]
    hb = nb // 2
    fetch = pltpu.make_async_copy(listed, lst, sem)
    fetch.start()
    fill_partners(lo, a_ref, 0, hb)
    fill_partners(hi, a_ref, hb + nb, hb)
    a_ref[hb : hb + nb] = a_own[...]

    def own_tile(i, _):
        st = own[0:5, lanes(i)]
        x, s = st[0:3], st[4:5]
        one = jnp.ones_like(s)
        zero = jnp.zeros_like(s)
        c = LOG2E / (s * s)
        b_ref[i] = stack_b(jnp.concatenate([2.0 * c * x, -c, one, zero, -c * norm_sq(x), zero], 0))
        return 0

    lax.fori_loop(0, nb, own_tile, 0, unroll=4)
    b_ref[nb] = jnp.zeros((KF, BLK), bf16)
    acc[...] = jnp.zeros_like(acc)

    def work(at, size):
        for g in range(size):
            code = lst[at + g]
            e = jnp.dot(a_ref[code & 255], b_ref[code >> 8], preferred_element_type=f32)
            acc[code >> 8] += jnp.exp2(e).reshape(BLK // 8, 8, BLK).sum(0)

    fetch.wait()
    for_groups(lst, work)
    d = acc[0:nb].sum(1) * (1.0 / (NP * BLK))
    den[...] = d
    term[...] = jnp.exp2(jnp.log2(d) * (-1.0 / 3.0))


def density(own, lo, hi, a_own, lst):
    nb = a_own.shape[0]
    return pl.pallas_call(
        density_kernel,
        out_shape=[
            jax.ShapeDtypeStruct((nb, BLK), f32),
            jax.ShapeDtypeStruct((nb, BLK), f32),
            jax.ShapeDtypeStruct((2 * nb, BLK, KF), bf16),
        ],
        in_specs=[VM, VM, VM, VM, AN],
        out_specs=[VM] * 3,
        scratch_shapes=[
            pltpu.VMEM((nb + 1, KF, BLK), bf16),
            pltpu.VMEM((nb + 1, 8, BLK), f32),
            pltpu.SMEM(lst.shape, i32),
            pltpu.SemaphoreType.DMA(()),
        ],
        compiler_params=pltpu.CompilerParams(vmem_limit_bytes=16 << 20),
        cost_estimate=pl.CostEstimate(flops=12 * nb * NP * BLK * BLK, bytes_accessed=8 << 20, transcendentals=nb * NP * BLK * BLK),
        name="density",
    )(own, lo, hi, a_own, lst)


def force_kernel(own, lo, hi, a_ref, town, tlo, thi, listed, out, b_ref, v_ref, acc, lst, sem):
    nb = town.shape[0]
    hb = nb // 2
    fetch = pltpu.make_async_copy(listed, lst, sem)
    fetch.start()

    def sources(src, t, at, count):
        def body(i, _):
            st = src[0:5, lanes(i)]
            x, m = st[0:3], st[3:4]
            mt = m * t[pl.ds(i, 1), :]
            v = jnp.concatenate([m, m * x, mt, mt * x], 0)
            h = v.astype(bf16).astype(f32)
            v_ref[at + i] = jnp.concatenate([h, v - h], 0).astype(bf16)
            return 0

        lax.fori_loop(0, count, body, 0, unroll=8)

    sources(lo, tlo, 0, hb)
    sources(own, town, hb, nb)
    sources(hi, thi, hb + nb, hb)

    def own_tile(i, _):
        st = own[0:5, lanes(i)]
        x, s = st[0:3], st[4:5]
        one = jnp.ones_like(s)
        z = jnp.zeros_like(s)
        dist = jnp.concatenate([(2.0 * LOG2E) * x, -LOG2E * one, z, z, -LOG2E * norm_sq(x), z], 0)
        spread = jnp.concatenate([z, z, z, z, z, one, 0.5 * s * s, z], 0)
        b_ref[i, :, 0:BLK] = stack_b(dist)
        b_ref[i, :, BLK : 2 * BLK] = stack_b(spread)
        return 0

    lax.fori_loop(0, nb, own_tile, 0, unroll=4)
    b_ref[nb] = jnp.ones((KF, 2 * BLK), bf16)
    acc[...] = jnp.zeros_like(acc)
    def work(at, size):
        lag = min(8, size // 4)
        codes = [lst[at + g] for g in range(size)]
        forms = {}
        weights = {}
        for step in range(size + 2 * lag):
            if step < size:
                code = codes[step]
                forms[step] = jnp.dot(a_ref[code & 255], b_ref[code >> 8], preferred_element_type=f32)
            g = step - lag
            if 0 <= g < size:
                e = forms.pop(g)
                r = pl.reciprocal(e[:, BLK : 2 * BLK], approx=True)
                weights[g] = (jnp.exp2(e[:, 0:BLK] * r) * r).astype(bf16)
            g = step - 2 * lag
            if 0 <= g < size:
                code = codes[g]
                acc[code >> 8] += jnp.dot(v_ref[code & 255], weights.pop(g), preferred_element_type=f32)

    fetch.wait()
    for_groups(lst, work)

    def finish(i, _):
        a = acc[i]
        s = a[0:8] + a[8:16]
        x = own[0:3, lanes(i)]
        t = town[pl.ds(i, 1), :]
        f = t * (x * s[0:1] - s[1:4]) + (x * s[4:5] - s[5:8])
        out[:, lanes(i)] = f * (2.0 / (NP * BLK))
        return 0

    lax.fori_loop(0, nb, finish, 0, unroll=8)


def force(own, lo, hi, a, town, tlo, thi, lst):
    nb = town.shape[0]
    return pl.pallas_call(
        force_kernel,
        out_shape=jax.ShapeDtypeStruct((3, nb * BLK), f32),
        in_specs=[VM] * 7 + [AN],
        out_specs=VM,
        scratch_shapes=[
            pltpu.VMEM((nb + 1, KF, 2 * BLK), bf16),
            pltpu.VMEM((2 * nb, 16, BLK), bf16),
            pltpu.VMEM((nb + 1, 16, BLK), f32),
            pltpu.SMEM(lst.shape, i32),
            pltpu.SemaphoreType.DMA(()),
        ],
        compiler_params=pltpu.CompilerParams(vmem_limit_bytes=16 << 20),
        cost_estimate=pl.CostEstimate(flops=24 * nb * NP * BLK * BLK, bytes_accessed=8 << 20, transcendentals=2 * nb * NP * BLK * BLK),
        name="force",
    )(own, lo, hi, a, town, tlo, thi, lst)


def on_device(positions, mass, smooth, cell_y, cell_z, cic_frac, pair_blocks, pair_count):
    hb = pair_blocks.shape[0] // 2
    slabs = lax.axis_size("slab")
    cols = lax.axis_size("col")
    up = [(i, (i + 1) % slabs) for i in range(slabs)]
    down = [((i + 1) % slabs, i) for i in range(slabs)]
    right = [(i, (i + 1) % cols) for i in range(cols)]
    own, tail, head, lst = pack(
        positions, mass, smooth, cell_y, cell_z, cic_frac, pair_blocks.T, pair_count
    )
    lo = lax.ppermute(tail, "slab", up)
    hi = lax.ppermute(head, "slab", down)
    grid, rim, a_own = deposit_own(own)
    den, term, a = density(own, lo, hi, a_own, lst)
    tlo = lax.ppermute(term[hb:], "slab", up)
    thi = lax.ppermute(term[:hb], "slab", down)
    grid, rim, edge_row = deposit_in(lo, grid, rim, term)
    rows = lax.ppermute(rim[:XP], "col", right)
    acceleration = force(own, lo, hi, a, term, tlo, thi, lst)
    rows, acceleration = lax.optimization_barrier((rows, acceleration))
    grid = lax.dynamic_update_slice(grid, edge_row + rows[:, None], (0, 0, 0))
    return den.reshape(-1), acceleration, grid


def solution(mesh):
    return jax.shard_map(
        on_device,
        mesh=mesh,
        in_specs=(
            P(None, ("slab", "col")),
            P(("slab", "col")),
            P(("slab", "col")),
            P(("slab", "col")),
            P(("slab", "col")),
            P(None, ("slab", "col")),
            P(("slab", "col"), None),
            P(("slab", "col")),
        ),
        out_specs=(P(("slab", "col")), P(None, ("slab", "col")), P("slab", "col", None)),
        check_vma=False,
    )
```

```python
import functools

import jax
import jax.numpy as jnp
from jax import lax
from jax.experimental import pallas as pl
from jax.experimental.pallas import tpu as pltpu
from jax.sharding import PartitionSpec as P

BLK = 128
NP = 9
XP = 2
MYD = 128
MZ = 1024
LOG2E = 1.4426950408889634
KF = 48
GROUP = 64
REST = 16
SPAN = 1024
ZB = 1024

f32 = jnp.float32
bf16 = jnp.bfloat16
i16 = jnp.int16
i32 = jnp.int32

VM = pl.BlockSpec(memory_space=pltpu.VMEM)
SM = pl.BlockSpec(memory_space=pltpu.SMEM)
AN = pl.BlockSpec(memory_space=pl.ANY)
HB = pl.BlockSpec(memory_space=pltpu.HBM)
NT = (((1,), (1,)), ((), ()))


def lanes(i, width=BLK):
    return pl.ds(pl.multiple_of(i * width, BLK), width)


def pack_kernel(pos, mass, smooth, cy, cz, frac, pairs, counts, own, tail, head, lst, spairs, scounts, vpos, vmass, vsmooth, vcy, vcz, vfrac, sems):
    half = own.shape[1] // 2
    moves = (
        (pos, vpos),
        (mass, vmass),
        (smooth, vsmooth),
        (cy, vcy),
        (cz, vcz),
        (frac, vfrac),
        (pairs, spairs),
        (counts, scounts),
    )
    copies = [pltpu.make_async_copy(src, dst, sems.at[k]) for k, (src, dst) in enumerate(moves)]
    for copy in copies:
        copy.start()
    for copy in copies[-2:] + copies[:-2]:
        copy.wait()
    nb = counts.shape[1]
    hb = nb // 2
    for b in range(hb):
        for n, (row, partner) in enumerate(((b, hb + b), (b, nb + b), (hb + b, hb + b), (hb + b, nb + b))):
            lst[4 * b + n] = i32(row * 256 + partner)
    at = i32(2 * nb)
    for b in range(nb):
        for n, k in enumerate((1 if b < hb else 2,) + tuple(range(3, NP))):
            lst[at + n] = spairs[k, b] + b * 256
        at = at + scounts[0, b] - 2
    for k in range(REST):
        lst[at + k] = i32(nb * 256)
    lst[lst.shape[0] - 1] = at
    own[0:3] = vpos[...]
    own[3:4] = vmass[...]
    own[4:5] = vsmooth[...]
    own[5:6] = vcy[...].astype(f32)
    own[6:7] = vcz[...].astype(f32)
    own[7:10] = vfrac[...]
    tail[...] = own[:, half:]
    head[...] = own[0:5, :half]


def pack(positions, mass, smooth, cell_y, cell_z, cic_frac, pairs, counts):
    n = mass.shape[0]
    nb = counts.shape[0]
    return pl.pallas_call(
        pack_kernel,
        out_shape=[
            jax.ShapeDtypeStruct((10, n), f32),
            jax.ShapeDtypeStruct((10, n // 2), f32),
            jax.ShapeDtypeStruct((5, n // 2), f32),
            jax.ShapeDtypeStruct((nb * NP + NP + 2 * REST,), i32),
        ],
        in_specs=[HB] * 8,
        out_specs=[VM] * 3 + [SM],
        scratch_shapes=[
            pltpu.SMEM((NP, nb), i32),
            pltpu.SMEM((1, nb), i32),
            pltpu.VMEM((3, n), f32),
            pltpu.VMEM((1, n), f32),
            pltpu.VMEM((1, n), f32),
            pltpu.VMEM((1, n), i32),
            pltpu.VMEM((1, n), i32),
            pltpu.VMEM((3, n), f32),
            pltpu.SemaphoreType.DMA((8,)),
        ],
        name="pack",
    )(positions, mass[None], smooth[None], cell_y[None], cell_z[None], cic_frac, pairs, counts[None])


def split3(x):
    h = x.astype(bf16).astype(f32)
    r = x - h
    m = r.astype(bf16).astype(f32)
    return h, m, r - m


def stack_a(x):
    h, m, l = split3(x)
    return jnp.concatenate([h, h, m, m, h, l], 0).astype(bf16)


def stack_b(x):
    h, m, l = split3(x)
    return jnp.concatenate([h, m, h, m, l, h], 0).astype(bf16)


def norm_sq(x):
    return x[0:1] * x[0:1] + x[1:2] * x[1:2] + x[2:3] * x[2:3]


def partner_tile(st):
    x, m, s = st[0:3], st[3:4], st[4:5]
    one = jnp.ones_like(m)
    rows = jnp.concatenate([x, norm_sq(x), jnp.log2(m), 0.5 * s * s, one, jnp.zeros_like(one)], 0)
    return stack_a(rows).T


def density_tile(st):
    x, s = st[0:3], st[4:5]
    one = jnp.ones_like(s)
    zero = jnp.zeros_like(s)
    c = LOG2E / (s * s)
    return stack_b(jnp.concatenate([2.0 * c * x, -c, one, zero, -c * norm_sq(x), zero], 0))


def column_sums(e):
    return jnp.exp2(e).reshape(e.shape[0] // 8, 8, BLK).sum(0)


def fill_partners(src, a_ref, at, count):
    step = min(16, count)

    def body(i, _):
        for u in range(step):
            b = i * step + u
            a_ref[at + b] = partner_tile(src[0:5, lanes(b)])
        return 0

    lax.fori_loop(0, count // step, body, 0)


def hat_parts(c, low, high, wrap):
    odd = (c & 1) != 0
    row = lax.broadcasted_iota(i32, (16, c.shape[1]), 0)
    even_row = (row & 1) == 0
    at = jnp.where(even_row, ((c + 1) >> 1) & wrap, c >> 1)
    value = jnp.where(even_row, jnp.where(odd, high, low), jnp.where(odd, low, high))
    hit = jnp.where((at & 7) == (row >> 1), value, 0.0)
    return (at >> 3).astype(f32), hit.astype(bf16)


def hat_table(top, hit, tiles):
    zero = jnp.zeros_like(hit)
    return jnp.concatenate([jnp.where(top == jnp.full((), t, bf16), hit, zero) for t in range(tiles)], 0)


def row_table(cy, mx, fy):
    high = mx * fy
    top, hit = hat_parts(cy, mx * (1.0 - fy), high, MYD - 1)
    edge = jnp.where(cy == MYD - 1, high, 0.0).astype(bf16)
    return hat_table(top.astype(bf16), hit, MYD // 16), edge


def fill_tables(st, at, k, planes, edges, rows_ref, top_ref, hit_ref):
    span = pl.ds(k * SPAN, SPAN)
    s = st[:, pl.ds(at + k * SPAN, SPAN)]
    m, cy, cz, fx, fy, fz = s[3:4], s[5:6].astype(i32), s[6:7].astype(i32), s[7:8], s[8:9], s[9:10]
    row = lax.broadcasted_iota(i32, (16, SPAN), 0)
    rim = jnp.zeros((16, SPAN), bf16)
    for n, (plane, edge_at) in enumerate(zip(planes, edges)):
        main, edge = row_table(cy, m * (fx if plane else 1.0 - fx), fy)
        rows_ref[n * MYD : (n + 1) * MYD, span] = main
        rim = jnp.where(row == edge_at, edge.astype(f32), rim.astype(f32)).astype(bf16)
    rows_ref[len(planes) * MYD : len(planes) * MYD + 16, span] = rim
    top, hit = hat_parts(cz, 1.0 - fz, fz, MZ // 2 - 1)
    top_ref[:, span] = top
    hit_ref[:, span] = hit


def table_scratch(planes, n):
    return [
        pltpu.VMEM((planes * MYD + 16, n), bf16),
        pltpu.VMEM((16, n), f32),
        pltpu.VMEM((16, n), bf16),
    ]


def deposit_dot(z, rows_ref, top_ref, hit_ref):
    tiles = ZB // 16
    top = (top_ref[...] - (z * tiles).astype(f32)).astype(bf16)
    return lax.dot_general(rows_ref[...], hat_table(top, hit_ref[...], tiles), NT, preferred_element_type=f32)


def deposit_dot_one(z, rows_ref, top_ref, hit_ref):
    tiles = ZB // 16
    top = (top_ref[...] - (z * tiles).astype(f32)).astype(bf16)
    u = lax.dot_general(hat_table(top, hit_ref[...], tiles), rows_ref[...], NT, preferred_element_type=f32)
    return u.T


def deposit_own_kernel(st, grid, rim, a_own, start, rows1, top1, hit1, rows2, top2, hit2):
    n = st.shape[1]
    half = n // 2
    nb = a_own.shape[0]
    hb = nb // 2
    fill_partners(st, a_own, 0, nb)

    def own_pairs(i, _):
        for u in range(8):
            b = i * 8 + u
            w = jnp.concatenate([density_tile(st[0:5, lanes(b)]), density_tile(st[0:5, lanes(b + hb)])], 1)
            e = jnp.dot(jnp.concatenate([a_own[b], a_own[b + hb]], 0), w, preferred_element_type=f32)
            start[b] = column_sums(e[:, 0:BLK])
            start[b + hb] = column_sums(e[:, BLK : 2 * BLK])
        return 0

    lax.fori_loop(0, hb // 8, own_pairs, 0)
    for k in range(half // SPAN):
        fill_tables(st, 0, k, (0, 1), (0, 1), rows1, top1, hit1)
        fill_tables(st, half, k, (0,), (1,), rows2, top2, hit2)

    def body(z, _):
        at = lanes(z, ZB)
        u = deposit_dot(z, rows1, top1, hit1)
        v = deposit_dot_one(z, rows2, top2, hit2)
        grid[0, :, at] = u[0:MYD]
        grid[1, :, at] = u[MYD : 2 * MYD] + v[0:MYD]
        rim[:, at] = u[2 * MYD : 2 * MYD + 8] + v[MYD : MYD + 8]
        return 0

    lax.fori_loop(0, MZ // ZB, body, 0)


def deposit_own(st):
    nb = st.shape[1] // BLK
    return pl.pallas_call(
        deposit_own_kernel,
        out_shape=[
            jax.ShapeDtypeStruct((XP, MYD, MZ), f32),
            jax.ShapeDtypeStruct((8, MZ), f32),
            jax.ShapeDtypeStruct((nb, BLK, KF), bf16),
            jax.ShapeDtypeStruct((nb, 8, BLK), f32),
        ],
        in_specs=[VM],
        out_specs=[VM] * 4,
        scratch_shapes=table_scratch(2, st.shape[1] // 2) + table_scratch(1, st.shape[1] // 2),
        compiler_params=pltpu.CompilerParams(vmem_limit_bytes=16 << 20),
        cost_estimate=pl.CostEstimate(flops=4 * st.shape[1] * MYD * MZ, bytes_accessed=4 << 20, transcendentals=0),
        name="deposit_own",
    )(st)


def deposit_in_kernel(st, g_in, r_in, after, grid, rim, edge_row, rows, top, hit):
    for k in range(st.shape[1] // SPAN):
        fill_tables(st, 0, k, (1,), (0,), rows, top, hit)

    def body(z, _):
        at = lanes(z, ZB)
        u = deposit_dot_one(z, rows, top, hit)
        grid[0, :, at] = g_in[0, :, at] + u[0:MYD]
        grid[1, :, at] = g_in[1, :, at]
        rim[:, at] = r_in[:, at] + u[MYD : MYD + 8]
        return 0

    lax.fori_loop(0, MZ // ZB, body, 0)
    edge_row[...] = grid[:, 0:1, :]


def deposit_in(st, g, r, after):
    return pl.pallas_call(
        deposit_in_kernel,
        out_shape=[
            jax.ShapeDtypeStruct((XP, MYD, MZ), f32),
            jax.ShapeDtypeStruct((8, MZ), f32),
            jax.ShapeDtypeStruct((XP, 1, MZ), f32),
        ],
        in_specs=[VM, VM, VM, AN],
        out_specs=[VM] * 3,
        scratch_shapes=table_scratch(1, st.shape[1]),
        compiler_params=pltpu.CompilerParams(vmem_limit_bytes=16 << 20),
        cost_estimate=pl.CostEstimate(flops=2 * st.shape[1] * MYD * MZ, bytes_accessed=4 << 20, transcendentals=0),
        name="deposit_in",
    )(st, g, r, after)


def for_groups(lst, work, skip):
    live = lst[lst.shape[0] - 1] - skip
    full = live // GROUP

    def whole(it, _):
        work(skip + it * GROUP, GROUP)
        return 0

    def rest(it, _):
        work(skip + full * GROUP + it * REST, REST)
        return 0

    lax.fori_loop(0, full, whole, 0)
    lax.fori_loop(0, (live - full * GROUP + REST - 1) // REST, rest, 0)


def density_kernel(own, lo, hi, a_own, start, listed, den, term, a_ref, b_ref, acc, lst, sem):
    nb = den.shape[0]
    hb = nb // 2
    fetch = pltpu.make_async_copy(listed, lst, sem)
    fetch.start()
    fill_partners(lo, a_ref, 0, hb)
    fill_partners(hi, a_ref, hb + nb, hb)
    a_ref[hb : hb + nb] = a_own[...]

    def own_tile(i, _):
        b_ref[i] = density_tile(own[0:5, lanes(i)])
        return 0

    lax.fori_loop(0, nb, own_tile, 0, unroll=4)
    b_ref[nb] = jnp.zeros((KF, BLK), bf16)
    acc[0:nb] = start[...]
    acc[nb] = jnp.zeros((8, BLK), f32)

    def work(at, size):
        for g in range(size):
            code = lst[at + g]
            e = jnp.dot(a_ref[code & 255], b_ref[code >> 8], preferred_element_type=f32)
            acc[code >> 8] += column_sums(e)

    fetch.wait()
    for_groups(lst, work, 2 * nb)
    d = acc[0:nb].sum(1) * (1.0 / (NP * BLK))
    den[...] = d
    term[...] = jnp.exp2(jnp.log2(d) * (-1.0 / 3.0))


def density(own, lo, hi, a_own, start, lst):
    nb = a_own.shape[0]
    return pl.pallas_call(
        density_kernel,
        out_shape=[
            jax.ShapeDtypeStruct((nb, BLK), f32),
            jax.ShapeDtypeStruct((nb, BLK), f32),
            jax.ShapeDtypeStruct((2 * nb, BLK, KF), bf16),
        ],
        in_specs=[VM, VM, VM, VM, VM, AN],
        out_specs=[VM] * 3,
        scratch_shapes=[
            pltpu.VMEM((nb + 1, KF, BLK), bf16),
            pltpu.VMEM((nb + 1, 8, BLK), f32),
            pltpu.SMEM(lst.shape, i32),
            pltpu.SemaphoreType.DMA(()),
        ],
        compiler_params=pltpu.CompilerParams(vmem_limit_bytes=16 << 20),
        cost_estimate=pl.CostEstimate(flops=12 * nb * NP * BLK * BLK, bytes_accessed=8 << 20, transcendentals=nb * NP * BLK * BLK),
        name="density",
    )(own, lo, hi, a_own, start, lst)


def force_kernel(own, lo, hi, a_ref, town, tlo, thi, listed, out, b_ref, v_ref, acc, lst, sem):
    nb = town.shape[0]
    hb = nb // 2
    fetch = pltpu.make_async_copy(listed, lst, sem)
    fetch.start()

    def sources(src, t, at, count):
        def body(i, _):
            st = src[0:5, lanes(i)]
            x, m = st[0:3], st[3:4]
            mt = m * t[pl.ds(i, 1), :]
            v = jnp.concatenate([m, m * x, mt, mt * x], 0)
            h = v.astype(bf16).astype(f32)
            v_ref[at + i] = jnp.concatenate([h, v - h], 0).astype(bf16)
            return 0

        lax.fori_loop(0, count, body, 0, unroll=8)

    sources(lo, tlo, 0, hb)
    sources(own, town, hb, nb)
    sources(hi, thi, hb + nb, hb)

    def own_tile(i, _):
        st = own[0:5, lanes(i)]
        x, s = st[0:3], st[4:5]
        one = jnp.ones_like(s)
        z = jnp.zeros_like(s)
        dist = jnp.concatenate([(2.0 * LOG2E) * x, -LOG2E * one, z, z, -LOG2E * norm_sq(x), z], 0)
        spread = jnp.concatenate([z, z, z, z, z, one, 0.5 * s * s, z], 0)
        b_ref[i, :, 0:BLK] = stack_b(dist)
        b_ref[i, :, BLK : 2 * BLK] = stack_b(spread)
        return 0

    lax.fori_loop(0, nb, own_tile, 0, unroll=4)
    b_ref[nb] = jnp.ones((KF, 2 * BLK), bf16)
    acc[...] = jnp.zeros_like(acc)
    def work(at, size):
        lag = min(8, size // 4)
        codes = [lst[at + g] for g in range(size)]
        forms = {}
        weights = {}
        for step in range(size + 2 * lag):
            if step < size:
                code = codes[step]
                forms[step] = jnp.dot(a_ref[code & 255], b_ref[code >> 8], preferred_element_type=f32)
            g = step - lag
            if 0 <= g < size:
                e = forms.pop(g)
                r = pl.reciprocal(e[:, BLK : 2 * BLK], approx=True)
                weights[g] = (jnp.exp2(e[:, 0:BLK] * r) * r).astype(bf16)
            g = step - 2 * lag
            if 0 <= g < size:
                code = codes[g]
                acc[code >> 8] += jnp.dot(v_ref[code & 255], weights.pop(g), preferred_element_type=f32)

    fetch.wait()
    for_groups(lst, work, 0)

    def finish(i, _):
        a = acc[i]
        s = a[0:8] + a[8:16]
        x = own[0:3, lanes(i)]
        t = town[pl.ds(i, 1), :]
        f = t * (x * s[0:1] - s[1:4]) + (x * s[4:5] - s[5:8])
        out[:, lanes(i)] = f * (2.0 / (NP * BLK))
        return 0

    lax.fori_loop(0, nb, finish, 0, unroll=8)


def force(own, lo, hi, a, town, tlo, thi, lst):
    nb = town.shape[0]
    return pl.pallas_call(
        force_kernel,
        out_shape=jax.ShapeDtypeStruct((3, nb * BLK), f32),
        in_specs=[VM] * 7 + [AN],
        out_specs=VM,
        scratch_shapes=[
            pltpu.VMEM((nb + 1, KF, 2 * BLK), bf16),
            pltpu.VMEM((2 * nb, 16, BLK), bf16),
            pltpu.VMEM((nb + 1, 16, BLK), f32),
            pltpu.SMEM(lst.shape, i32),
            pltpu.SemaphoreType.DMA(()),
        ],
        compiler_params=pltpu.CompilerParams(vmem_limit_bytes=16 << 20),
        cost_estimate=pl.CostEstimate(flops=24 * nb * NP * BLK * BLK, bytes_accessed=8 << 20, transcendentals=2 * nb * NP * BLK * BLK),
        name="force",
    )(own, lo, hi, a, town, tlo, thi, lst)


def on_device(positions, mass, smooth, cell_y, cell_z, cic_frac, pair_blocks, pair_count):
    hb = pair_blocks.shape[0] // 2
    slabs = lax.axis_size("slab")
    cols = lax.axis_size("col")
    up = [(i, (i + 1) % slabs) for i in range(slabs)]
    down = [((i + 1) % slabs, i) for i in range(slabs)]
    right = [(i, (i + 1) % cols) for i in range(cols)]
    own, tail, head, lst = pack(
        positions, mass, smooth, cell_y, cell_z, cic_frac, pair_blocks.T, pair_count
    )
    lo = lax.ppermute(tail, "slab", up)
    hi = lax.ppermute(head, "slab", down)
    grid, rim, a_own, start = deposit_own(own)
    den, term, a = density(own, lo, hi, a_own, start, lst)
    tlo = lax.ppermute(term[hb:], "slab", up)
    thi = lax.ppermute(term[:hb], "slab", down)
    grid, rim, edge_row = deposit_in(lo, grid, rim, term)
    rows = lax.ppermute(rim[:XP], "col", right)
    acceleration = force(own, lo, hi, a, term, tlo, thi, lst)
    rows, acceleration = lax.optimization_barrier((rows, acceleration))
    grid = lax.dynamic_update_slice(grid, edge_row + rows[:, None], (0, 0, 0))
    return den.reshape(-1), acceleration, grid


def solution(mesh):
    return jax.shard_map(
        on_device,
        mesh=mesh,
        in_specs=(
            P(None, ("slab", "col")),
            P(("slab", "col")),
            P(("slab", "col")),
            P(("slab", "col")),
            P(("slab", "col")),
            P(None, ("slab", "col")),
            P(("slab", "col"), None),
            P(("slab", "col")),
        ),
        out_specs=(P(("slab", "col")), P(None, ("slab", "col")), P("slab", "col", None)),
        check_vma=False,
    )
```

```python
import functools

import jax
import jax.numpy as jnp
from jax import lax
from jax.experimental import pallas as pl
from jax.experimental.pallas import tpu as pltpu
from jax.sharding import PartitionSpec as P

BLK = 128
NP = 9
XP = 2
MYD = 128
MZ = 1024
LOG2E = 1.4426950408889634
KF = 48
GROUP = 64
REST = 16
SPAN = 1024
ZB = 1024

f32 = jnp.float32
bf16 = jnp.bfloat16
i16 = jnp.int16
i32 = jnp.int32

VM = pl.BlockSpec(memory_space=pltpu.VMEM)
SM = pl.BlockSpec(memory_space=pltpu.SMEM)
AN = pl.BlockSpec(memory_space=pl.ANY)
HB = pl.BlockSpec(memory_space=pltpu.HBM)
NT = (((1,), (1,)), ((), ()))


def lanes(i, width=BLK):
    return pl.ds(pl.multiple_of(i * width, BLK), width)


def pack_kernel(pos, mass, smooth, cy, cz, frac, pairs, counts, own_out, tail, head_out, lst, spairs, scounts, vpos, vmass, vsmooth, vcy, vcz, vfrac, own, head, sems):
    half = tail.shape[1]
    moves = (
        (pos, vpos),
        (mass, vmass),
        (smooth, vsmooth),
        (cy, vcy),
        (cz, vcz),
        (frac, vfrac),
        (pairs, spairs),
        (counts, scounts),
    )
    copies = [pltpu.make_async_copy(src, dst, sems.at[k]) for k, (src, dst) in enumerate(moves)]
    for copy in copies:
        copy.start()
    for copy in copies[-2:] + copies[:-2]:
        copy.wait()
    own[0:3] = vpos[...]
    own[3:4] = vmass[...]
    own[4:5] = vsmooth[...]
    own[5:6] = vcy[...].astype(f32)
    own[6:7] = vcz[...].astype(f32)
    own[7:10] = vfrac[...]
    head[...] = own[0:5, :half]
    sends = [
        pltpu.make_async_copy(own.at[:, pl.ds(half, half)], tail, sems.at[8]),
        pltpu.make_async_copy(head, head_out, sems.at[9]),
        pltpu.make_async_copy(own, own_out, sems.at[10]),
    ]
    for copy in sends:
        copy.start()
    nb = counts.shape[1]
    hb = nb // 2
    for b in range(hb):
        for n, (row, partner) in enumerate(((b, hb + b), (b, nb + b), (hb + b, hb + b), (hb + b, nb + b))):
            lst[4 * b + n] = i32(row * 256 + partner)
    at = i32(2 * nb)
    for b in range(nb):
        for n, k in enumerate((1 if b < hb else 2,) + tuple(range(3, NP))):
            lst[at + n] = spairs[k, b] + b * 256
        at = at + scounts[0, b] - 2
    for k in range(REST):
        lst[at + k] = i32(nb * 256)
    lst[lst.shape[0] - 1] = at
    for copy in sends:
        copy.wait()


def pack(positions, mass, smooth, cell_y, cell_z, cic_frac, pairs, counts):
    n = mass.shape[0]
    nb = counts.shape[0]
    return pl.pallas_call(
        pack_kernel,
        out_shape=[
            jax.ShapeDtypeStruct((10, n), f32),
            jax.ShapeDtypeStruct((10, n // 2), f32),
            jax.ShapeDtypeStruct((5, n // 2), f32),
            jax.ShapeDtypeStruct((nb * NP + NP + 2 * REST,), i32),
        ],
        in_specs=[HB] * 8,
        out_specs=[HB] * 3 + [SM],
        scratch_shapes=[
            pltpu.SMEM((NP, nb), i32),
            pltpu.SMEM((1, nb), i32),
            pltpu.VMEM((3, n), f32),
            pltpu.VMEM((1, n), f32),
            pltpu.VMEM((1, n), f32),
            pltpu.VMEM((1, n), i32),
            pltpu.VMEM((1, n), i32),
            pltpu.VMEM((3, n), f32),
            pltpu.VMEM((10, n), f32),
            pltpu.VMEM((5, n // 2), f32),
            pltpu.SemaphoreType.DMA((11,)),
        ],
        name="pack",
    )(positions, mass[None], smooth[None], cell_y[None], cell_z[None], cic_frac, pairs, counts[None])


def split3(x):
    h = x.astype(bf16).astype(f32)
    r = x - h
    m = r.astype(bf16).astype(f32)
    return h, m, r - m


def stack_a(x):
    h, m, l = split3(x)
    return jnp.concatenate([h, h, m, m, h, l], 0).astype(bf16)


def stack_b(x):
    h, m, l = split3(x)
    return jnp.concatenate([h, m, h, m, l, h], 0).astype(bf16)


def norm_sq(x):
    return x[0:1] * x[0:1] + x[1:2] * x[1:2] + x[2:3] * x[2:3]


def partner_tile(st):
    x, m, s = st[0:3], st[3:4], st[4:5]
    one = jnp.ones_like(m)
    rows = jnp.concatenate([x, norm_sq(x), jnp.log2(m), 0.5 * s * s, one, jnp.zeros_like(one)], 0)
    return stack_a(rows).T


def density_tile(st):
    x, s = st[0:3], st[4:5]
    one = jnp.ones_like(s)
    zero = jnp.zeros_like(s)
    c = LOG2E / (s * s)
    return stack_b(jnp.concatenate([2.0 * c * x, -c, one, zero, -c * norm_sq(x), zero], 0))


def column_sums(e):
    return jnp.exp2(e).reshape(e.shape[0] // 8, 8, BLK).sum(0)


def fill_partners(src, a_ref, at, count):
    step = min(16, count)

    def body(i, _):
        for u in range(step):
            b = i * step + u
            a_ref[at + b] = partner_tile(src[0:5, lanes(b)])
        return 0

    lax.fori_loop(0, count // step, body, 0)


def hat_parts(c, low, high, wrap):
    odd = (c & 1) != 0
    row = lax.broadcasted_iota(i32, (16, c.shape[1]), 0)
    even_row = (row & 1) == 0
    at = jnp.where(even_row, ((c + 1) >> 1) & wrap, c >> 1)
    value = jnp.where(even_row, jnp.where(odd, high, low), jnp.where(odd, low, high))
    hit = jnp.where((at & 7) == (row >> 1), value, 0.0)
    return (at >> 3).astype(f32), hit.astype(bf16)


def hat_table(top, hit, tiles):
    zero = jnp.zeros_like(hit)
    return jnp.concatenate([jnp.where(top == jnp.full((), t, bf16), hit, zero) for t in range(tiles)], 0)


def row_table(cy, mx, fy):
    high = mx * fy
    top, hit = hat_parts(cy, mx * (1.0 - fy), high, MYD - 1)
    edge = jnp.where(cy == MYD - 1, high, 0.0).astype(bf16)
    return hat_table(top.astype(bf16), hit, MYD // 16), edge


def fill_tables(st, at, k, planes, edges, rows_ref, top_ref, hit_ref):
    span = pl.ds(k * SPAN, SPAN)
    s = st[:, pl.ds(at + k * SPAN, SPAN)]
    m, cy, cz, fx, fy, fz = s[3:4], s[5:6].astype(i32), s[6:7].astype(i32), s[7:8], s[8:9], s[9:10]
    row = lax.broadcasted_iota(i32, (16, SPAN), 0)
    rim = jnp.zeros((16, SPAN), bf16)
    for n, (plane, edge_at) in enumerate(zip(planes, edges)):
        main, edge = row_table(cy, m * (fx if plane else 1.0 - fx), fy)
        rows_ref[n * MYD : (n + 1) * MYD, span] = main
        rim = jnp.where(row == edge_at, edge.astype(f32), rim.astype(f32)).astype(bf16)
    rows_ref[len(planes) * MYD : len(planes) * MYD + 16, span] = rim
    top, hit = hat_parts(cz, 1.0 - fz, fz, MZ // 2 - 1)
    top_ref[:, span] = top
    hit_ref[:, span] = hit


def table_scratch(planes, n):
    return [
        pltpu.VMEM((planes * MYD + 16, n), bf16),
        pltpu.VMEM((16, n), f32),
        pltpu.VMEM((16, n), bf16),
    ]


def deposit_dot(z, rows_ref, top_ref, hit_ref):
    tiles = ZB // 16
    top = (top_ref[...] - (z * tiles).astype(f32)).astype(bf16)
    return lax.dot_general(rows_ref[...], hat_table(top, hit_ref[...], tiles), NT, preferred_element_type=f32)


def deposit_dot_one(z, rows_ref, top_ref, hit_ref):
    tiles = ZB // 16
    top = (top_ref[...] - (z * tiles).astype(f32)).astype(bf16)
    u = lax.dot_general(hat_table(top, hit_ref[...], tiles), rows_ref[...], NT, preferred_element_type=f32)
    return u.T


def deposit_own_kernel(st, grid, rim, a_own, start, rows1, top1, hit1, rows2, top2, hit2):
    n = st.shape[1]
    half = n // 2
    nb = a_own.shape[0]
    hb = nb // 2
    fill_partners(st, a_own, 0, nb)

    def own_pairs(i, _):
        for u in range(8):
            b = i * 8 + u
            w = jnp.concatenate([density_tile(st[0:5, lanes(b)]), density_tile(st[0:5, lanes(b + hb)])], 1)
            e = jnp.dot(jnp.concatenate([a_own[b], a_own[b + hb]], 0), w, preferred_element_type=f32)
            start[b] = column_sums(e[:, 0:BLK])
            start[b + hb] = column_sums(e[:, BLK : 2 * BLK])
        return 0

    lax.fori_loop(0, hb // 8, own_pairs, 0)
    for k in range(half // SPAN):
        fill_tables(st, 0, k, (0, 1), (0, 1), rows1, top1, hit1)
        fill_tables(st, half, k, (0,), (1,), rows2, top2, hit2)

    def body(z, _):
        at = lanes(z, ZB)
        u = deposit_dot(z, rows1, top1, hit1)
        v = deposit_dot_one(z, rows2, top2, hit2)
        grid[0, :, at] = u[0:MYD]
        grid[1, :, at] = u[MYD : 2 * MYD] + v[0:MYD]
        rim[:, at] = u[2 * MYD : 2 * MYD + 8] + v[MYD : MYD + 8]
        return 0

    lax.fori_loop(0, MZ // ZB, body, 0)


def deposit_own(st):
    nb = st.shape[1] // BLK
    return pl.pallas_call(
        deposit_own_kernel,
        out_shape=[
            jax.ShapeDtypeStruct((XP, MYD, MZ), f32),
            jax.ShapeDtypeStruct((8, MZ), f32),
            jax.ShapeDtypeStruct((nb, BLK, KF), bf16),
            jax.ShapeDtypeStruct((nb, 8, BLK), f32),
        ],
        in_specs=[VM],
        out_specs=[VM] * 4,
        scratch_shapes=table_scratch(2, st.shape[1] // 2) + table_scratch(1, st.shape[1] // 2),
        compiler_params=pltpu.CompilerParams(vmem_limit_bytes=16 << 20),
        cost_estimate=pl.CostEstimate(flops=4 * st.shape[1] * MYD * MZ, bytes_accessed=4 << 20, transcendentals=0),
        name="deposit_own",
    )(st)


def deposit_in_kernel(st, g_in, r_in, after, grid, rim, edge_row, rows, top, hit):
    for k in range(st.shape[1] // SPAN):
        fill_tables(st, 0, k, (1,), (0,), rows, top, hit)

    def body(z, _):
        at = lanes(z, ZB)
        u = deposit_dot_one(z, rows, top, hit)
        grid[0, :, at] = g_in[0, :, at] + u[0:MYD]
        grid[1, :, at] = g_in[1, :, at]
        rim[:, at] = r_in[:, at] + u[MYD : MYD + 8]
        return 0

    lax.fori_loop(0, MZ // ZB, body, 0)
    edge_row[...] = grid[:, 0:1, :]


def deposit_in(st, g, r, after):
    return pl.pallas_call(
        deposit_in_kernel,
        out_shape=[
            jax.ShapeDtypeStruct((XP, MYD, MZ), f32),
            jax.ShapeDtypeStruct((8, MZ), f32),
            jax.ShapeDtypeStruct((XP, 1, MZ), f32),
        ],
        in_specs=[VM, VM, VM, AN],
        out_specs=[VM] * 3,
        scratch_shapes=table_scratch(1, st.shape[1]),
        compiler_params=pltpu.CompilerParams(vmem_limit_bytes=16 << 20),
        cost_estimate=pl.CostEstimate(flops=2 * st.shape[1] * MYD * MZ, bytes_accessed=4 << 20, transcendentals=0),
        name="deposit_in",
    )(st, g, r, after)


def for_groups(lst, work, skip):
    live = lst[lst.shape[0] - 1] - skip
    full = live // GROUP

    def whole(it, _):
        work(skip + it * GROUP, GROUP)
        return 0

    def rest(it, _):
        work(skip + full * GROUP + it * REST, REST)
        return 0

    lax.fori_loop(0, full, whole, 0)
    lax.fori_loop(0, (live - full * GROUP + REST - 1) // REST, rest, 0)


def density_kernel(own, lo, hi, a_own, start, listed, den, term, a_ref, b_ref, acc, lst, sem):
    nb = den.shape[0]
    hb = nb // 2
    fetch = pltpu.make_async_copy(listed, lst, sem)
    fetch.start()
    fill_partners(lo, a_ref, 0, hb)
    fill_partners(hi, a_ref, hb + nb, hb)
    a_ref[hb : hb + nb] = a_own[...]

    def own_tile(i, _):
        b_ref[i] = density_tile(own[0:5, lanes(i)])
        return 0

    lax.fori_loop(0, nb, own_tile, 0, unroll=4)
    b_ref[nb] = jnp.zeros((KF, BLK), bf16)
    acc[0:nb] = start[...]
    acc[nb] = jnp.zeros((8, BLK), f32)

    def work(at, size):
        for g in range(size):
            code = lst[at + g]
            e = jnp.dot(a_ref[code & 255], b_ref[code >> 8], preferred_element_type=f32)
            acc[code >> 8] += column_sums(e)

    fetch.wait()
    for_groups(lst, work, 2 * nb)
    d = acc[0:nb].sum(1) * (1.0 / (NP * BLK))
    den[...] = d
    term[...] = jnp.exp2(jnp.log2(d) * (-1.0 / 3.0))


def density(own, lo, hi, a_own, start, lst):
    nb = a_own.shape[0]
    return pl.pallas_call(
        density_kernel,
        out_shape=[
            jax.ShapeDtypeStruct((nb, BLK), f32),
            jax.ShapeDtypeStruct((nb, BLK), f32),
            jax.ShapeDtypeStruct((2 * nb, BLK, KF), bf16),
        ],
        in_specs=[VM, VM, VM, VM, VM, AN],
        out_specs=[VM] * 3,
        scratch_shapes=[
            pltpu.VMEM((nb + 1, KF, BLK), bf16),
            pltpu.VMEM((nb + 1, 8, BLK), f32),
            pltpu.SMEM(lst.shape, i32),
            pltpu.SemaphoreType.DMA(()),
        ],
        compiler_params=pltpu.CompilerParams(vmem_limit_bytes=16 << 20),
        cost_estimate=pl.CostEstimate(flops=12 * nb * NP * BLK * BLK, bytes_accessed=8 << 20, transcendentals=nb * NP * BLK * BLK),
        name="density",
    )(own, lo, hi, a_own, start, lst)


def force_kernel(own, lo, hi, a_ref, town, tlo, thi, listed, out, b_ref, v_ref, acc, lst, sem):
    nb = town.shape[0]
    hb = nb // 2
    fetch = pltpu.make_async_copy(listed, lst, sem)
    fetch.start()

    def sources(src, t, at, count):
        def body(i, _):
            st = src[0:5, lanes(i)]
            x, m = st[0:3], st[3:4]
            mt = m * t[pl.ds(i, 1), :]
            v = jnp.concatenate([m, m * x, mt, mt * x], 0)
            h = v.astype(bf16).astype(f32)
            v_ref[at + i] = jnp.concatenate([h, v - h], 0).astype(bf16)
            return 0

        lax.fori_loop(0, count, body, 0, unroll=8)

    sources(lo, tlo, 0, hb)
    sources(own, town, hb, nb)
    sources(hi, thi, hb + nb, hb)

    def own_tile(i, _):
        st = own[0:5, lanes(i)]
        x, s = st[0:3], st[4:5]
        one = jnp.ones_like(s)
        z = jnp.zeros_like(s)
        dist = jnp.concatenate([(2.0 * LOG2E) * x, -LOG2E * one, z, z, -LOG2E * norm_sq(x), z], 0)
        spread = jnp.concatenate([z, z, z, z, z, one, 0.5 * s * s, z], 0)
        b_ref[i, :, 0:BLK] = stack_b(dist)
        b_ref[i, :, BLK : 2 * BLK] = stack_b(spread)
        return 0

    lax.fori_loop(0, nb, own_tile, 0, unroll=4)
    b_ref[nb] = jnp.ones((KF, 2 * BLK), bf16)
    acc[...] = jnp.zeros_like(acc)
    def work(at, size):
        lag = min(8, size // 4)
        codes = [lst[at + g] for g in range(size)]
        forms = {}
        weights = {}
        for step in range(size + 2 * lag):
            if step < size:
                code = codes[step]
                forms[step] = jnp.dot(a_ref[code & 255], b_ref[code >> 8], preferred_element_type=f32)
            g = step - lag
            if 0 <= g < size:
                e = forms.pop(g)
                r = pl.reciprocal(e[:, BLK : 2 * BLK], approx=True)
                weights[g] = (jnp.exp2(e[:, 0:BLK] * r) * r).astype(bf16)
            g = step - 2 * lag
            if 0 <= g < size:
                code = codes[g]
                acc[code >> 8] += jnp.dot(v_ref[code & 255], weights.pop(g), preferred_element_type=f32)

    fetch.wait()
    for_groups(lst, work, 0)

    def finish(i, _):
        a = acc[i]
        s = a[0:8] + a[8:16]
        x = own[0:3, lanes(i)]
        t = town[pl.ds(i, 1), :]
        f = t * (x * s[0:1] - s[1:4]) + (x * s[4:5] - s[5:8])
        out[:, lanes(i)] = f * (2.0 / (NP * BLK))
        return 0

    lax.fori_loop(0, nb, finish, 0, unroll=8)


def force(own, lo, hi, a, town, tlo, thi, lst):
    nb = town.shape[0]
    return pl.pallas_call(
        force_kernel,
        out_shape=jax.ShapeDtypeStruct((3, nb * BLK), f32),
        in_specs=[VM] * 7 + [AN],
        out_specs=VM,
        scratch_shapes=[
            pltpu.VMEM((nb + 1, KF, 2 * BLK), bf16),
            pltpu.VMEM((2 * nb, 16, BLK), bf16),
            pltpu.VMEM((nb + 1, 16, BLK), f32),
            pltpu.SMEM(lst.shape, i32),
            pltpu.SemaphoreType.DMA(()),
        ],
        compiler_params=pltpu.CompilerParams(vmem_limit_bytes=16 << 20),
        cost_estimate=pl.CostEstimate(flops=24 * nb * NP * BLK * BLK, bytes_accessed=8 << 20, transcendentals=2 * nb * NP * BLK * BLK),
        name="force",
    )(own, lo, hi, a, town, tlo, thi, lst)


def on_device(positions, mass, smooth, cell_y, cell_z, cic_frac, pair_blocks, pair_count):
    hb = pair_blocks.shape[0] // 2
    slabs = lax.axis_size("slab")
    cols = lax.axis_size("col")
    up = [(i, (i + 1) % slabs) for i in range(slabs)]
    down = [((i + 1) % slabs, i) for i in range(slabs)]
    right = [(i, (i + 1) % cols) for i in range(cols)]
    own, tail, head, lst = pack(
        positions, mass, smooth, cell_y, cell_z, cic_frac, pair_blocks.T, pair_count
    )
    lo = lax.ppermute(tail, "slab", up)
    hi = lax.ppermute(head, "slab", down)
    grid, rim, a_own, start = deposit_own(own)
    den, term, a = density(own, lo, hi, a_own, start, lst)
    tlo = lax.ppermute(term[hb:], "slab", up)
    thi = lax.ppermute(term[:hb], "slab", down)
    grid, rim, edge_row = deposit_in(lo, grid, rim, term)
    rows = lax.ppermute(rim[:XP], "col", right)
    acceleration = force(own, lo, hi, a, term, tlo, thi, lst)
    rows, acceleration = lax.optimization_barrier((rows, acceleration))
    grid = lax.dynamic_update_slice(grid, edge_row + rows[:, None], (0, 0, 0))
    return den.reshape(-1), acceleration, grid


def solution(mesh):
    return jax.shard_map(
        on_device,
        mesh=mesh,
        in_specs=(
            P(None, ("slab", "col")),
            P(("slab", "col")),
            P(("slab", "col")),
            P(("slab", "col")),
            P(("slab", "col")),
            P(None, ("slab", "col")),
            P(("slab", "col"), None),
            P(("slab", "col")),
        ),
        out_specs=(P(("slab", "col")), P(None, ("slab", "col")), P("slab", "col", None)),
        check_vma=False,
    )
```
